128 devices in a mesh: ctx: 16 (over z, x), head: 2 (over y_hi), dp: 4 (over y_lo, core).
Axes of the slice: x: 4, y: 4 (y_hi: 2, y_lo: 2; y = y_hi * 2 + y_lo), z: 4, core: 2. Of those that a mesh axis runs over, the one named last changes fastest.
Arguments:
- queries: bfloat16 [4, 2048, 5120], P('dp', 'ctx', 'head'), may hold values from -200 to 200
- keys: bfloat16 [4, 16384, 1024], P('dp', 'ctx', 'head'), may hold values from -6 to 6
- start_block: int32 [4], P('dp'), may hold values from 0 to 224, as said below
- lengths: int32 [4], P('dp'), may hold values from 2048 to 16384, as said below
- gate_query: bfloat16 [8, 640, 128], P('head'), may hold values from -2 to 2
- gate_key: bfloat16 [8, 384, 128], P('head'), may hold values from -0.3125 to 0.3125
Outputs:
- grad_query: float32 [8, 640, 128], P('head')
- grad_key: float32 [8, 384, 128], P('head')
- block_loss: float32 [4, 8], P('dp', 'head')
The draws below stay inside these ranges and needn't reach their ends.
Inputs may be any that keep to these rules, and one draw needn't show every extreme that they name: The span's 32 blocks lie inside the context: start_block + 32 <= 256. Every query token of the span lies before the sequence's length: lengths >= 64 * (start_block + 32).
All inputs are finite; a program needn't handle non-finite values.
Results may differ from the reference program's by a relative error of at most 0.0003.
Values may be sent and summed in bfloat16 or wider, within the bound.
No kernel may reach another device: no remote copies, remote signals or barrier semaphores. Data moves between devices by JAX's collectives and lax.ppermute only.
A program may use at most 320 MiB of HBM per device.

```python
import math
import jax
import jax.numpy as jnp
from jax import lax

HQ = 40
KVH = 8
HD = 128
GATE_DIM = 128
BLK = 64
GROUP = 5
QLEN = 2048
CTX = 16384
QB = 32
CB = 256
SEQS = 4


def span_layout(key):
    order = jax.random.permutation(jax.random.fold_in(key, 11), SEQS)
    starts = jax.random.randint(jax.random.fold_in(key, 12), (SEQS,), 0, CB - QB + 1)
    starts = jnp.where(order == 0, CB - QB, jnp.where(order == 1, 0, starts))
    lowest = (starts + QB) * BLK
    spread = jax.random.randint(jax.random.fold_in(key, 13), (SEQS,), 0, 1 << 20)
    seq_lengths = lowest + spread % (CTX - lowest + 1)
    seq_lengths = jnp.where(order == 1, QB * BLK, jnp.where(order == 2, CTX, seq_lengths))
    return (starts.astype(jnp.int32), seq_lengths.astype(jnp.int32))


def base_keys(key):
    return jax.random.truncated_normal(jax.random.fold_in(key, 21), -6.0, 6.0, (SEQS, CTX, KVH * HD), jnp.float32)


def draw_start_block(key, part):
    return span_layout(key)[0]


def draw_lengths(key, part):
    return span_layout(key)[1]


def draw_keys(key, part):
    return base_keys(key).astype(jnp.bfloat16)


def draw_queries(key, part):
    key = jax.random.fold_in(key, 31)
    values = jax.random.truncated_normal(key, -6.0, 6.0, (SEQS, QLEN, HQ * HD), jnp.float32)
    return values.astype(jnp.bfloat16)


def block_scale(stream_key, extent, split, smallest, largest):
    def one(dim, shards_of):
        draws = jax.random.uniform(jax.random.fold_in(jax.random.fold_in(stream_key, 6), dim), (shards_of,), jnp.float32, smallest / len(split), largest / len(split))
        return jnp.repeat(jnp.exp(draws), extent[dim] // shards_of).reshape((-1,) + (1,) * (len(extent) - dim - 1))

    gain = one(*split[0])
    for cut in split[1:]:
        gain = gain * one(*cut)
    return gain


def bell_draw(rng, dims, scale, most, shards=(), held_as=jnp.bfloat16):
    gain = block_scale(rng, dims, shards, -0.22, 0.18) if shards else 1.0
    entries = jax.random.normal(rng, dims, jnp.float32) * scale * gain
    return jnp.minimum(jnp.maximum(entries, -most), most).astype(held_as)


def setup_inputs(seed: int = 0) -> dict:
    splits = jax.random.split(jax.random.key(seed), 7)
    return {
        "queries": draw_queries(jax.random.fold_in(splits[6], 71), 0),
        "keys": draw_keys(jax.random.fold_in(splits[6], 71), 0),
        "start_block": draw_start_block(jax.random.fold_in(splits[6], 71), 0),
        "lengths": draw_lengths(jax.random.fold_in(splits[6], 71), 0),
        "gate_query": bell_draw(splits[4], (KVH, GROUP * HD, GATE_DIM), (GROUP * HD // 64) ** -0.5, 2.0, ((0, 2),)),
        "gate_key": bell_draw(splits[5], (KVH, 3 * HD, GATE_DIM), (3 * HD) ** -0.5, 0.3125, ((0, 2),)),
    }


NEG = -1e30
HIGH = lax.Precision.HIGHEST


def teacher_rows(rows, key_group, first_row, seq_length):
    row_count = rows.shape[0]
    ctx_len = key_group.shape[0]
    scores = jnp.einsum("qhd,kd->hqk", rows.astype(jnp.float32), key_group.astype(jnp.float32)) * (rows.shape[2] ** -0.5)
    query_pos = first_row + jnp.arange(row_count, dtype=jnp.int32)
    key_pos = jnp.arange(ctx_len, dtype=jnp.int32)
    visible = (key_pos[None, :] <= query_pos[:, None]) & (key_pos[None, :] < seq_length)
    masked = jnp.where(visible[None], scores, NEG)
    row_top = jnp.max(masked, axis=2, keepdims=True)
    weights = jnp.where(visible[None], jnp.exp(masked - row_top), 0.0)
    probs = weights / jnp.sum(weights, axis=2, keepdims=True)
    pooled = probs.reshape(GROUP, row_count // BLK, BLK, ctx_len // BLK, BLK).max(axis=(2, 4))
    return jnp.mean(pooled, axis=0)


def pool_queries(grouped):
    groups, row_count, width = grouped.shape
    return jnp.mean(grouped.astype(jnp.float32).reshape(groups, row_count // BLK, BLK, width), axis=2)


def pool_keys(grouped):
    groups, row_count, width = grouped.shape
    blocks = grouped.astype(jnp.float32).reshape(groups, row_count // BLK, BLK, width)
    return jnp.concatenate([blocks.max(axis=2), blocks.min(axis=2), blocks.mean(axis=2)], axis=2)


def gate_logits(pooled_q, pooled_k, weight_q, weight_k, q_blocks, k_blocks, seq_length):
    proj_q = jnp.einsum("gqc,gcd->gqd", pooled_q, weight_q.astype(jnp.float32), precision=HIGH)
    proj_k = jnp.einsum("gkc,gcd->gkd", pooled_k, weight_k.astype(jnp.float32), precision=HIGH)
    logits = jnp.einsum("gqd,gkd->gqk", proj_q, proj_k, precision=HIGH) * (proj_q.shape[2] ** -0.5)
    visible = (k_blocks[None, :] <= q_blocks[:, None]) & (k_blocks[None, :] * BLK < seq_length)
    masked = jnp.where(visible[None], logits, NEG)
    return proj_q, proj_k, masked, visible


def gate_grads(pooled_q, pooled_k, proj_q, proj_k, masked, visible, gate_top, gate_sum, target, blocks_q):
    gate_prob = jnp.where(visible[None], jnp.exp(masked - gate_top) / gate_sum, 0.0)
    log_gate = masked - gate_top - jnp.log(gate_sum)
    terms = jax.scipy.special.xlogy(target, target) - jnp.where(visible[None], target * log_gate, 0.0)
    kl_loss = jnp.sum(terms, axis=(1, 2)) / blocks_q
    slope = (gate_prob - target) / blocks_q
    scale_factor = proj_q.shape[2] ** -0.5
    slope_q = jnp.einsum("gqk,gkd->gqd", slope, proj_k, precision=HIGH) * scale_factor
    slope_k = jnp.einsum("gqk,gqd->gkd", slope, proj_q, precision=HIGH) * scale_factor
    grad_q = jnp.einsum("gqc,gqd->gcd", pooled_q, slope_q, precision=HIGH)
    grad_k = jnp.einsum("gkc,gkd->gcd", pooled_k, slope_k, precision=HIGH)
    return kl_loss, grad_q, grad_k


def reference(queries, keys, start_block, lengths, gate_query, gate_key):
    row_block = math.gcd(QLEN, 512)
    block_steps = QLEN // row_block
    grad_query = jnp.zeros(gate_query.shape, jnp.float32)
    grad_key = jnp.zeros(gate_key.shape, jnp.float32)
    losses = []
    for seq in range(SEQS):
        start_blk = start_block[seq]
        seq_length = lengths[seq]
        query_heads = queries[seq].reshape(QLEN, KVH, GROUP, HD).transpose(1, 0, 2, 3)
        key_heads = keys[seq].reshape(CTX, KVH, HD).transpose(1, 0, 2)

        def per_group(operands):
            query_group, key_group = operands

            def per_rows(block_index):
                rows = lax.dynamic_slice_in_dim(query_group, block_index * row_block, row_block, 0)
                return teacher_rows(rows, key_group, start_blk * BLK + block_index * row_block, seq_length)

            return lax.map(per_rows, jnp.arange(block_steps, dtype=jnp.int32)).reshape(QB, CB)

        teacher = lax.map(per_group, (query_heads, key_heads))
        target = teacher / jnp.sum(teacher, axis=2, keepdims=True)
        pooled_q = pool_queries(queries[seq].reshape(QLEN, KVH, GROUP * HD).transpose(1, 0, 2))
        pooled_k = pool_keys(key_heads)
        q_blocks = start_blk + jnp.arange(QB, dtype=jnp.int32)
        k_blocks = jnp.arange(CB, dtype=jnp.int32)
        proj_q, proj_k, masked, visible = gate_logits(pooled_q, pooled_k, gate_query, gate_key, q_blocks, k_blocks, seq_length)
        gate_top = jnp.max(masked, axis=2, keepdims=True)
        gate_sum = jnp.sum(jnp.where(visible[None], jnp.exp(masked - gate_top), 0.0), axis=2, keepdims=True)
        kl_loss, grad_q, grad_k = gate_grads(pooled_q, pooled_k, proj_q, proj_k, masked, visible, gate_top, gate_sum, target, QB)
        grad_query = grad_query + grad_q
        grad_key = grad_key + grad_k
        losses.append(kl_loss)
    return grad_query, grad_key, jnp.stack(losses)
```

```python
import functools
import math

import jax
import jax.numpy as jnp
from jax import lax
from jax.experimental import pallas as pl
from jax.experimental.pallas import tpu as pltpu
from jax.sharding import Mesh, PartitionSpec as P

BLK = 64
GROUP = 5
HD = 128
QB = 32
NEG = -1e30
FLOOR = -1e20
KT = 512
KB = KT // BLK
SCALE = HD ** -0.5
SCALE2 = SCALE * math.log2(math.e)
VMEM = 56 * 2 ** 20
F32 = jnp.float32
BF16 = jnp.bfloat16
NT = (((1,), (1,)), ((), ()))
TN = (((0,), (0,)), ((), ()))
NN = (((1,), (0,)), ((), ()))


def split2(x):
    hi = x.astype(BF16)
    return hi, (x - hi.astype(F32)).astype(BF16)


def mm(a, b, dims):
    return lax.dot_general(a, b, dims, preferred_element_type=F32)


def dot2(a, b, dims):
    hi, lo = split2(a)
    return mm(hi, b, dims) + mm(lo, b, dims)


def dot3(a, b, dims):
    ah, al = split2(a)
    bh, bl = split2(b)
    return mm(ah, bh, dims) + (mm(ah, bl, dims) + mm(al, bh, dims))


def block_update(s, m, l, floor):
    rt = s.shape[1]
    tops = []
    for j in range(KB):
        sj = s[j * BLK:(j + 1) * BLK]
        top = sj.reshape(8, 8, rt).max(axis=0).max(axis=0, keepdims=True)
        tops.append(top)
        if floor:
            top = jnp.maximum(top, FLOOR)
        if m is None:
            m = top
            l = jnp.exp2(sj - m).reshape(8, 8, rt).sum(axis=0)
        else:
            new = jnp.maximum(m, top)
            l = l * jnp.exp2(m - new) + jnp.exp2(sj - new).reshape(8, 8, rt).sum(axis=0)
            m = new
    return jnp.concatenate(tops, axis=0), m, l


def scores_kernel(pos_ref, *refs, q_rows, k_rows, shards):
    nq, nk = len(q_rows), len(k_rows)
    q_refs, k_refs = refs[:nq], refs[nq:nq + nk]
    bm_ref, ml_ref, qs, m_s, l_s = refs[nq + nk:]
    rt = sum(q_rows)
    tiles = [(p, o) for p in range(nk) for o in range(0, k_rows[p], KT)]
    q_at, t_at = shards, shards + nq
    for h in range(GROUP):
        for p in range(nq):
            x = q_refs[p][:, h * HD:(h + 1) * HD].astype(F32) * SCALE2
            hi, lo = split2(x)
            at = pl.multiple_of(pos_ref[q_at + p], BLK)
            qs[h, pl.ds(at, q_rows[p]), :] = jnp.concatenate([hi, lo], axis=1)
    q_pos = [pos_ref[i] for i in range(shards)]
    low = functools.reduce(jnp.minimum, q_pos)
    high = functools.reduce(jnp.maximum, q_pos) + 1
    kp = [pos_ref[t_at + 2 * t] for t in range(len(tiles))]
    out = [pl.multiple_of(pos_ref[t_at + 2 * t + 1], KB) for t in range(len(tiles))]
    full = functools.reduce(jnp.maximum, kp) + KB - 1 < low

    def scores(t, h):
        p, o = tiles[t]
        k = k_refs[p][o:o + KT, :]
        return mm(jnp.concatenate([k, k], axis=1), qs[h], NT)

    def head(h, _):
        @pl.when(full)
        def _():
            m = l = None
            for t in range(len(tiles)):
                top, m, l = block_update(scores(t, h), m, l, False)
                bm_ref[0, h, pl.ds(out[t], KB), :] = top
            ml_ref[0, h, 0:1, :] = m
            ml_ref[0, h, 1:2, :] = l.sum(axis=0, keepdims=True)

        @pl.when(jnp.logical_not(full))
        def _():
            m_s[...] = jnp.full(m_s.shape, FLOOR, F32)
            l_s[...] = jnp.zeros(l_s.shape, F32)
            lane = lax.broadcasted_iota(jnp.int32, (1, rt), 1)
            q_row = lane % 128
            for i in range(shards):
                q_row = q_row + jnp.where(lane // 128 == i, q_pos[i] * BLK, 0)
            for t in range(len(tiles)):
                none = kp[t] > high

                @pl.when(jnp.logical_not(none))
                def _():
                    k_row = kp[t] * BLK + lax.broadcasted_iota(jnp.int32, (KT, rt), 0)
                    s = jnp.where(k_row <= q_row, scores(t, h), NEG)
                    top, m, l = block_update(s, m_s[...], l_s[...], True)
                    bm_ref[0, h, pl.ds(out[t], KB), :] = top
                    m_s[...] = m
                    l_s[...] = l

                @pl.when(none)
                def _():
                    bm_ref[0, h, pl.ds(out[t], KB), :] = jnp.full((KB, rt), NEG, F32)

            ml_ref[0, h, 0:1, :] = m_s[...]
            ml_ref[0, h, 1:2, :] = l_s[...].sum(axis=0, keepdims=True)

        return 0

    lax.fori_loop(0, GROUP, head, 0)


def block_scores(pos, q_parts, k_parts, shards):
    q_rows = [q.shape[0] for q in q_parts]
    k_rows = [k.shape[0] for k in k_parts]
    rt, kn = sum(q_rows), sum(k_rows)
    groups = k_parts[0].shape[1] // HD
    return pl.pallas_call(
        functools.partial(scores_kernel, q_rows=q_rows, k_rows=k_rows, shards=shards),
        grid_spec=pltpu.PrefetchScalarGridSpec(
            num_scalar_prefetch=1,
            grid=(groups,),
            in_specs=[pl.BlockSpec((r, GROUP * HD), lambda g, p: (0, g)) for r in q_rows]
            + [pl.BlockSpec((r, HD), lambda g, p: (0, g)) for r in k_rows],
            out_specs=[
                pl.BlockSpec((1, GROUP, kn // BLK, rt), lambda g, p: (g, 0, 0, 0)),
                pl.BlockSpec((1, GROUP, 2, rt), lambda g, p: (g, 0, 0, 0)),
            ],
            scratch_shapes=[
                pltpu.VMEM((GROUP, rt, 2 * HD), BF16),
                pltpu.VMEM((1, rt), F32),
                pltpu.VMEM((8, rt), F32),
            ],
        ),
        out_shape=[
            jax.ShapeDtypeStruct((groups, GROUP, kn // BLK, rt), F32),
            jax.ShapeDtypeStruct((groups, GROUP, 2, rt), F32),
        ],
        compiler_params=pltpu.CompilerParams(vmem_limit_bytes=VMEM),
        cost_estimate=pl.CostEstimate(
            flops=4 * groups * GROUP * rt * kn * HD,
            bytes_accessed=4 * groups * GROUP * rt * kn // BLK,
            transcendentals=groups * GROUP * rt * kn,
        ),
        name="block_scores",
    )(pos, *q_parts, *k_parts)


def teacher_kernel(bm_ref, *refs):
    ml_refs, out_ref = refs[:-1], refs[-1]
    nb, rt = bm_ref.shape[2], bm_ref.shape[3]
    row = lax.broadcasted_iota(jnp.int32, (rt // BLK, rt), 0)
    lane = lax.broadcasted_iota(jnp.int32, (rt // BLK, rt), 1)
    pick = (lane == row * BLK).astype(BF16)
    halves = []
    for gg in range(2):
        total = None
        for h in range(GROUP):
            ms = [r[gg, h, 0:1, :] for r in ml_refs]
            m = functools.reduce(jnp.maximum, ms)
            l = sum(r[gg, h, 1:2, :] * jnp.exp2(mi - m) for r, mi in zip(ml_refs, ms))
            e = jnp.exp2(bm_ref[gg, h] - m) * (1.0 / l)
            cols = []
            for c in range(0, rt, 128):
                x = e[:, c:c + 128]
                for sh in (1, 2, 4, 8, 16, 32):
                    x = jnp.maximum(x, pltpu.roll(x, 128 - sh, 1))
                cols.append(x)
            x = jnp.concatenate(cols, axis=1)
            total = x if total is None else total + x
        total = total * (1.0 / GROUP)
        hi, lo = split2(total)
        lo2 = (total - hi.astype(F32) - lo.astype(F32)).astype(BF16)
        halves.append(mm(pick, hi, NT) + (mm(pick, lo, NT) + mm(pick, lo2, NT)))
    out_ref[0] = jnp.concatenate(halves, axis=1)


def teacher_blocks(bm, mls):
    groups, _, nb, rt = bm.shape
    return pl.pallas_call(
        teacher_kernel,
        grid=(groups // 2,),
        in_specs=[pl.BlockSpec((2, GROUP, nb, rt), lambda g: (g, 0, 0, 0))]
        + [pl.BlockSpec((2, GROUP, 2, rt), lambda g: (g, 0, 0, 0))] * len(mls),
        out_specs=pl.BlockSpec((1, rt // BLK, 2 * nb), lambda g: (g, 0, 0)),
        out_shape=jax.ShapeDtypeStruct((groups // 2, rt // BLK, 2 * nb), F32),
        compiler_params=pltpu.CompilerParams(vmem_limit_bytes=VMEM),
        name="teacher",
    )(bm, *mls)


def grads_kernel(pos_ref, pk0_ref, pk1_ref, pq_ref, t_ref, wq_ref, wk_ref, gq_ref, gk_ref, loss_ref):
    gp = pl.program_id(0)
    own_y, own_c = pos_ref[4], pos_ref[5]
    for gg in range(2):
        g = gp * 2 + gg
        d_qs, d_ks, pks = [], [], [[], [], []]
        loss_own = jnp.zeros((1, 1), F32)
        for si in range(4):
            crel, y = si // 2, si % 2
            c = jnp.where(own_c == crel, 0, 1)
            start = pos_ref[y * 2 + c]
            pk_ref = (pk0_ref, pk1_ref)[crel]
            parts = []
            for p in range(3):
                at = pl.multiple_of((g * 3 + p) * 16, 16)
                x = pk_ref[:, :, y, pl.ds(at, 16), :].reshape(256, 128)
                parts.append(x)
                pks[p].append(x)
            proj_k = sum(dot2(parts[p], wk_ref[gg, p * 128:(p + 1) * 128, :], NN) for p in range(3))
            pq = pq_ref[gg, si * QB:(si + 1) * QB, :]
            proj_q = dot2(pq, wq_ref[gg], NN)
            logits = dot3(proj_q, proj_k, NT) * SCALE
            row = lax.broadcasted_iota(jnp.int32, (QB, 256), 0)
            col = lax.broadcasted_iota(jnp.int32, (QB, 256), 1)
            a = (row % 8) // 2 * 8 + row // 8 * 2 + row % 2
            live = col <= start + a
            masked = jnp.where(live, logits, NEG)
            top = masked.max(axis=1, keepdims=True)
            ex = jnp.where(live, jnp.exp(masked - top), 0.0)
            total = ex.sum(axis=1, keepdims=True)
            gate = ex / total
            log_gate = masked - top - jnp.log(total)
            teacher = jnp.concatenate(
                [
                    jnp.concatenate(
                        [t_ref[z, x, y, c, 0, :, gg * 64:(gg + 1) * 64] for z in range(4)], axis=1
                    )
                    for x in range(4)
                ],
                axis=0,
            )
            target = teacher / teacher.sum(axis=1, keepdims=True)
            some = target > 0.0
            term = jnp.where(some, target * jnp.log(jnp.where(some, target, 1.0)), 0.0)
            term = term - jnp.where(live, target * log_gate, 0.0)
            if crel == 0:
                val = term.sum(axis=1, keepdims=True).sum(axis=0, keepdims=True) * (1.0 / QB)
                loss_own = loss_own + jnp.where(own_y == y, val, 0.0)
            slope = (gate - target) * (1.0 / QB)
            d_qs.append(dot3(slope, proj_k, NN) * SCALE)
            d_ks.append(dot3(slope, proj_q, TN) * SCALE)
        gq_ref[gg] = dot3(pq_ref[gg], jnp.concatenate(d_qs, axis=0), TN)
        d_k = jnp.concatenate(d_ks, axis=0)
        for p in range(3):
            gk_ref[gg, p * 128:(p + 1) * 128, :] = dot3(jnp.concatenate(pks[p], axis=0), d_k, TN)
        loss_ref[0, gg:gg + 1, :] = jnp.broadcast_to(loss_own, (1, 128))


def gate_gradients(pos, pk0, pk1, pq, teachers, wq, wk):
    groups = wq.shape[0]
    whole = lambda x: pl.BlockSpec(x.shape, lambda g, p: (0,) * x.ndim)
    pair = lambda x: pl.BlockSpec((2,) + x.shape[1:], lambda g, p: (g, 0, 0))
    return pl.pallas_call(
        grads_kernel,
        grid_spec=pltpu.PrefetchScalarGridSpec(
            num_scalar_prefetch=1,
            grid=(groups // 2,),
            in_specs=[
                whole(pk0),
                whole(pk1),
                pair(pq),
                pl.BlockSpec((4, 4, 2, 2, 1, 8, 128), lambda g, p: (0, 0, 0, 0, g, 0, 0)),
                pair(wq),
                pair(wk),
            ],
            out_specs=[
                pl.BlockSpec((2,) + wq.shape[1:], lambda g, p: (g, 0, 0)),
                pl.BlockSpec((2,) + wk.shape[1:], lambda g, p: (g, 0, 0)),
                pl.BlockSpec((1, 2, 128), lambda g, p: (g, 0, 0)),
            ],
        ),
        out_shape=[
            jax.ShapeDtypeStruct(wq.shape, F32),
            jax.ShapeDtypeStruct(wk.shape, F32),
            jax.ShapeDtypeStruct((groups // 2, 2, 128), F32),
        ],
        compiler_params=pltpu.CompilerParams(vmem_limit_bytes=VMEM),
        name="gate_gradients",
    )(pos, pk0, pk1, pq, teachers, wq, wk)


def shift(x, axis, by):
    return lax.ppermute(x, axis, [(i, (i + by) % 4) for i in range(4)])


def ring_parts(x, axis):
    half = x.shape[0] // 2
    before, after = shift(x, axis, 1), shift(x, axis, -1)
    return [x, before, after, shift(before[:half], axis, 1), shift(after[half:], axis, -1)]


def per_device(queries, keys, start_block, lengths, gate_query, gate_key):
    del lengths
    z, x = lax.axis_index("z"), lax.axis_index("x")
    y, c = lax.axis_index("y"), lax.axis_index("c")
    q, k = queries[0], keys[0]
    start = start_block[0]
    starts = lax.all_gather(start_block, ("y", "c"), tiled=True)
    q_mean = q.astype(F32).reshape(2, BLK, 4, GROUP, HD).mean(axis=1)
    kf = k.astype(F32).reshape(16, BLK, 4, HD)
    k_pool = jnp.stack([kf.max(axis=1), kf.min(axis=1), kf.mean(axis=1)], axis=2)
    pack = jnp.concatenate(
        [k_pool.transpose(1, 2, 0, 3).reshape(192, HD), q_mean.reshape(40, HD)], axis=0
    )
    pack = lax.all_gather(pack, "y")
    pack = lax.all_gather(pack, "x")
    pack = lax.all_gather(pack, "z")
    other = lax.ppermute(pack, "c", [(0, 1), (1, 0)])
    pq = jnp.stack([pack[..., 192:, :], other[..., 192:, :]])
    pq = pq.reshape(2, 4, 4, 2, 2, 4, GROUP * HD).transpose(5, 0, 3, 2, 1, 4, 6)
    pq = pq.reshape(4, 4 * QB, GROUP * HD)
    q_parts = ring_parts(q, "z")
    k_parts = ring_parts(k, "x")
    zs = [z, (z + 3) % 4, (z + 1) % 4, (z + 2) % 4]
    xs = [x, (x + 3) % 4, (x + 1) % 4, (x + 2) % 4]
    q_pos = [start + (zz * 4 + x) * 2 for zz in range(4)]
    q_at = [zs[0] * 128, zs[1] * 128, zs[2] * 128, zs[3] * 128, zs[3] * 128 + 64]
    t_at = []
    for xx in xs:
        for half in range(2):
            t_at += [(z * 4 + xx) * 16 + half * 8, xx * 16 + half * 8]
    pos = jnp.stack([jnp.asarray(v, jnp.int32) for v in q_pos + q_at + t_at])
    bm, ml = block_scores(pos, q_parts, k_parts, 4)
    mls = [ml, shift(ml, "z", 1), shift(ml, "z", -1), shift(ml, "z", 2)]
    teacher = teacher_blocks(bm, mls)
    teachers = lax.all_to_all(
        jnp.broadcast_to(teacher[None], (64,) + teacher.shape), ("z", "x", "y", "c"), 0, 0, tiled=True
    ).reshape((4, 4, 2, 2) + teacher.shape)
    pos2 = jnp.concatenate([starts, jnp.stack([y, c]).astype(jnp.int32)])
    grad_q, grad_k, loss = gate_gradients(pos2, pack, other, pq, teachers, gate_query, gate_key)
    return grad_q, grad_k, loss[:, :, 0].reshape(1, 4)


def solution(mesh):
    fine = Mesh(mesh.devices.reshape(4, 4, 2, 2, 2), ("z", "x", "h", "y", "c"))
    ctx, dp = ("z", "x"), ("y", "c")
    placed = (
        P(dp, ctx, "h"),
        P(dp, ctx, "h"),
        P(dp),
        P(dp),
        P("h", None, None),
        P("h", None, None),
    )
    return jax.shard_map(
        per_device,
        mesh=fine,
        in_specs=placed,
        out_specs=(P("h", None, None), P("h", None, None), P(dp, "h")),
        check_vma=False,
    )
```

```python
import functools
import math

import jax
import jax.numpy as jnp
from jax import lax
from jax.experimental import pallas as pl
from jax.experimental.pallas import tpu as pltpu
from jax.sharding import Mesh, PartitionSpec as P

BLK = 64
GROUP = 5
HD = 128
QB = 32
CB = 256
NEG = -1e30
FLOOR = -1e20
KT = 512
KB = KT // BLK
SAFE = 100.0
SCALE = HD ** -0.5
SCALE2 = SCALE * math.log2(math.e)
VMEM = 56 * 2 ** 20
F32 = jnp.float32
BF16 = jnp.bfloat16
NT = (((1,), (1,)), ((), ()))
TN = (((0,), (0,)), ((), ()))
NN = (((1,), (0,)), ((), ()))
PQ_AT = 256
START_AT = PQ_AT + 80
PACK = START_AT + 16


def split2(x):
    hi = x.astype(BF16)
    return hi, (x - hi.astype(F32)).astype(BF16)


def mm(a, b, dims=NN):
    return lax.dot_general(a, b, dims, preferred_element_type=F32)


def mm3(a, b, dims=NN):
    return mm(a[0], b[0], dims) + (mm(a[0], b[1], dims) + mm(a[1], b[0], dims))


def running(s, m, l):
    rt = s.shape[1]
    tops = []
    for j in range(s.shape[0] // BLK):
        sj = s[j * BLK:(j + 1) * BLK]
        top = sj.reshape(8, 8, rt).max(axis=0).max(axis=0, keepdims=True)
        tops.append(top)
        new = jnp.maximum(m, top)
        l = l * jnp.exp2(m - new) + jnp.exp2(sj - new).reshape(8, 8, rt).sum(axis=0)
        m = new
    return jnp.concatenate(tops, axis=0), m, l


def against(s, m):
    rt = s.shape[1]
    tops = s.reshape(s.shape[0] // BLK, 8, 8, rt).max(axis=1).max(axis=1)
    return tops, jnp.exp2(s - m).reshape(s.shape[0] // 8, 8, rt).sum(axis=0)


def scores_kernel(pos_ref, *refs, q_rows, prep, n_ml, k_rows, place):
    refs = list(refs)
    take = lambda n: [refs.pop(0) for _ in range(n)]
    q_refs = take(len(q_rows))
    k_refs = take(len(k_rows))
    ml_in = take(n_ml)
    bm_ref, ml_ref = take(2)
    rt = sum(q_rows)
    shards = rt // 128
    if prep:
        (qs,) = take(1)
        at = 0
        for r, n in zip(q_refs, q_rows):
            for h in range(GROUP):
                hi, lo = split2(r[:, h * HD:(h + 1) * HD].astype(F32) * SCALE2)
                to = h * rt + at
                qs[0, to:to + n, :HD] = hi
                qs[0, to:to + n, HD:] = lo
            at += n
        chunks = [(a, min(a + 512, GROUP * rt)) for a in range(0, GROUP * rt, 512)]
    else:
        chunks = [(h * rt, (h + 1) * rt) for h in range(GROUP)]

    def pieces(a, b, sizes):
        if len(sizes) == 1:
            return [(0, a, b)]
        got, at = [], 0
        h, a, b = a // rt, a % rt, (b - 1) % rt + 1
        for i, n in enumerate(sizes):
            lo, hi = max(a - at, 0), min(b - at, n)
            if lo < hi:
                got.append((i, h * n + lo, h * n + hi))
            at += n
        return got

    def join(parts, axis):
        return parts[0] if len(parts) == 1 else jnp.concatenate(parts, axis=axis)

    def rows_of(a, b):
        if prep:
            return qs[0, a:b, :]
        return join([q_refs[i][0, lo:hi, :] for i, lo, hi in pieces(a, b, q_rows)], 0)

    m_s, l_s, bad_s = refs
    tiles = [(p, o) for p in range(len(k_rows)) for o in range(0, k_rows[p], KT)]
    q_pos = [pos_ref[i] for i in range(shards)]
    kp = [pos_ref[shards + p] for p in range(len(k_rows))]
    low = functools.reduce(jnp.minimum, q_pos)
    ends = [kp[p] + k_rows[p] // BLK - 1 for p in range(len(k_rows))]
    full = functools.reduce(jnp.maximum, ends) < low

    def scores(t, a, b):
        p, o = tiles[t]
        k = k_refs[p][o:o + KT, :]
        return mm(jnp.concatenate([k, k], axis=1), rows_of(a, b), NT)

    def store(a, b, m, l, ref):
        l = l.sum(axis=0, keepdims=True)
        if ml_in:
            sizes = [b - a] if n_ml == 1 else q_rows
            old = join([ml_in[i][0, :, lo:hi] for i, lo, hi in pieces(a, b, sizes)], 1)
            new = jnp.maximum(m, old[0:1])
            l = l * jnp.exp2(ref - new) + old[1:2] * jnp.exp2(old[0:1] - new)
            m = new
        else:
            l = l * jnp.exp2(ref - m)
        if not place:
            ml_ref[0, 0:1, a:b] = m
            ml_ref[0, 1:2, a:b] = l
            return
        for i in range(shards):
            src = slice(i * 128, (i + 1) * 128)
            dst = pl.ds(pl.multiple_of(a + pos_ref[shards + len(k_rows) + i] * 128, 128), 128)
            ml_ref[0, 0:1, dst] = m[:, src]
            ml_ref[0, 1:2, dst] = l[:, src]

    @pl.when(full)
    def _():
        worst = []
        for a, b in chunks:
            m = l = big = None
            for t in range(len(tiles)):
                s = scores(t, a, b)
                if m is None:
                    m = s[:BLK].reshape(8, 8, b - a).max(axis=0).max(axis=0, keepdims=True)
                top, part = against(s, m)
                l = part if l is None else l + part
                bm_ref[0, t * KB:(t + 1) * KB, a:b] = top
                big = top if big is None else jnp.maximum(big, top)
            big = big.max(axis=0, keepdims=True)
            store(a, b, big, l, m)
            gap = big - m
            for c in range(0, b - a, 128):
                worst.append(gap[:, c:c + 128])
        bad_s[0] = jnp.max(functools.reduce(jnp.maximum, worst))

    @pl.when(jnp.logical_not(full))
    def _():
        bad_s[0] = 2 * SAFE

    @pl.when(bad_s[0] > SAFE)
    def _():
        m_s[...] = jnp.full(m_s.shape, FLOOR, F32)
        l_s[...] = jnp.zeros(l_s.shape, F32)
        for p in range(len(k_rows)):
            for u in range(0, rt, 256):
                w = min(256, rt - u)
                mine = q_pos[u // 128:(u + w) // 128]
                none = kp[p] > functools.reduce(jnp.maximum, mine) + 1

                @pl.when(none)
                def _():
                    for t, (tp, _) in enumerate(tiles):
                        for h in range(GROUP if tp == p else 0):
                            at = h * rt + u
                            bm_ref[0, t * KB:(t + 1) * KB, at:at + w] = jnp.full((KB, w), NEG, F32)

                @pl.when(jnp.logical_not(none))
                def _():
                    lane = lax.broadcasted_iota(jnp.int32, (8, w), 1)
                    q_row = lane % 128 - lax.broadcasted_iota(jnp.int32, (8, w), 0)
                    for i, v in enumerate(mine):
                        q_row = q_row + jnp.where(lane // 128 == i, v * BLK, 0)
                    q_row = q_row - kp[p] * BLK
                    for h in range(GROUP):
                        a, b = h * rt + u, h * rt + u + w
                        m, l = m_s[:, a:b], l_s[:, a:b]
                        for t, (tp, o) in enumerate(tiles):
                            if tp == p:
                                seen = jnp.concatenate([q_row >= o + i for i in range(0, KT, 8)], axis=0)
                                s = jnp.where(seen, scores(t, a, b), NEG)
                                top, m, l = running(s, m, l)
                                bm_ref[0, t * KB:(t + 1) * KB, a:b] = top
                        m_s[:, a:b] = m
                        l_s[:, a:b] = l
        for h in range(GROUP):
            a, b = h * rt, (h + 1) * rt
            store(a, b, m_s[:, a:b], l_s[:, a:b], m_s[:, a:b])


def block_scores(pos, q_parts, k_parts, ml_in=(), place=False):
    prep = not ml_in
    q_rows = [q.shape[0] if prep else q.shape[1] // GROUP for q in q_parts]
    k_rows = [k.shape[0] for k in k_parts]
    rt, kn = sum(q_rows), sum(k_rows)
    groups = k_parts[0].shape[1] // HD
    per_group = lambda *s: pl.BlockSpec((1,) + s, lambda g, p: (g,) + (0,) * len(s))
    if prep:
        q_specs = [pl.BlockSpec((r, GROUP * HD), lambda g, p: (0, g)) for r in q_rows]
    else:
        q_specs = [per_group(GROUP * r, 2 * HD) for r in q_rows]
    shapes = [(kn // BLK, GROUP * rt), (2, GROUP * rt)] + ([(GROUP * rt, 2 * HD)] if prep else [])
    types = [F32, F32, BF16]
    return pl.pallas_call(
        functools.partial(
            scores_kernel, q_rows=q_rows, prep=prep, n_ml=len(ml_in), k_rows=k_rows, place=place
        ),
        grid_spec=pltpu.PrefetchScalarGridSpec(
            num_scalar_prefetch=1,
            grid=(groups,),
            in_specs=q_specs
            + [pl.BlockSpec((r, HD), lambda g, p: (0, g)) for r in k_rows]
            + [per_group(*m.shape[1:]) for m in ml_in],
            out_specs=[per_group(*s) for s in shapes],
            scratch_shapes=[
                pltpu.VMEM((1, GROUP * rt), F32),
                pltpu.VMEM((8, GROUP * rt), F32),
                pltpu.SMEM((1,), F32),
            ],
        ),
        out_shape=[jax.ShapeDtypeStruct((groups,) + s, t) for s, t in zip(shapes, types)],
        compiler_params=pltpu.CompilerParams(vmem_limit_bytes=VMEM),
        cost_estimate=pl.CostEstimate(
            flops=4 * groups * GROUP * rt * kn * HD,
            bytes_accessed=4 * groups * GROUP * rt * kn // BLK,
            transcendentals=groups * GROUP * rt * kn,
        ),
        name="block_scores",
    )(pos, *q_parts, *k_parts, *ml_in)


def pool_kernel(start_ref, q_ref, k_ref, out_ref):
    groups = k_ref.shape[1] // HD
    for g in range(groups):
        x = k_ref[:, g * HD:(g + 1) * HD].astype(F32).reshape(16, BLK, HD)
        hi, lo = split2(x.sum(axis=1) * (1.0 / BLK))
        parts = [x.max(axis=1).astype(BF16), x.min(axis=1).astype(BF16), hi, lo]
        for p, part in enumerate(parts):
            out_ref[g * 64 + p * 16:g * 64 + p * 16 + 16, :] = part
    for p in range(GROUP):
        rows = []
        for g in range(groups):
            at = (g * GROUP + p) * HD
            x = q_ref[:, at:at + HD].astype(F32).reshape(2, BLK, HD)
            rows.append(x.sum(axis=1) * (1.0 / BLK))
        hi, lo = split2(jnp.concatenate(rows, axis=0))
        at = PQ_AT + p * 16
        out_ref[at:at + 16, :] = jnp.concatenate([hi.astype(F32), lo.astype(F32)], axis=0).astype(BF16)
    out_ref[START_AT:, :] = jnp.full((16, HD), start_ref[0].astype(F32), F32).astype(BF16)


def pool(start_block, q, k):
    return pl.pallas_call(
        pool_kernel,
        in_specs=[
            pl.BlockSpec(memory_space=pltpu.SMEM),
            pl.BlockSpec(memory_space=pltpu.VMEM),
            pl.BlockSpec(memory_space=pltpu.VMEM),
        ],
        out_specs=pl.BlockSpec(memory_space=pltpu.VMEM),
        out_shape=jax.ShapeDtypeStruct((PACK, HD), BF16),
        compiler_params=pltpu.CompilerParams(vmem_limit_bytes=VMEM),
        name="pool",
    )(start_block, q, k)


def teacher_kernel(pos_ref, *refs, n_bm):
    bm_refs, ml_refs, (out_ref, sc) = refs[:n_bm], refs[n_bm:-2], refs[-2:]
    z, x = pos_ref[0], pos_ref[1]
    a1, a2, mid, far = bm_refs
    totals = [None] * 4
    for h in range(GROUP):
        for r, off in enumerate((0, 3, 1, 2)):
            at = pl.multiple_of(h * 512 + ((z + off) & 3) * 128, 128)
            here = h * 512 + r * 128
            for gg in range(2):
                ms = [m[gg, 0:1, pl.ds(at, 128)] for m in ml_refs]
                m = functools.reduce(jnp.maximum, ms)
                l = sum(ref[gg, 1:2, pl.ds(at, 128)] * jnp.exp2(mi - m) for ref, mi in zip(ml_refs, ms))
                lse = m + jnp.log(l) * math.log2(math.e)
                own = a2[gg, :, h * 128:h * 128 + 128] if r == 3 else a1[gg, :, h * 384 + r * 128:h * 384 + r * 128 + 128]
                shards = [own, mid[gg, 0:16, here:here + 128], mid[gg, 16:32, here:here + 128], far[gg, :, here:here + 128]]
                for s, (v, xo) in enumerate(zip(shards, (0, 3, 1, 2))):
                    to = pl.multiple_of(gg * 64 + ((x + xo) & 3) * 16, 16)
                    sc[h * 4 + r, pl.ds(to, 16), :] = v - lse
    for h in range(GROUP):
        for r in range(4):
            t = sc[h * 4 + r].T
            top = jnp.exp2(t.reshape(2, BLK, 128).max(axis=1))
            totals[r] = top if h == 0 else totals[r] + top
    rows = jnp.concatenate([totals[0], totals[2], totals[3], totals[1]], axis=0)
    out_ref[0] = pltpu.roll(rows, 2 * z, 0) * (1.0 / GROUP)


def teacher_blocks(pos, bms, mls):
    groups = bms[0].shape[0]
    pair = lambda v: pl.BlockSpec((2,) + v.shape[1:], lambda g, p: (g, 0, 0))
    return pl.pallas_call(
        functools.partial(teacher_kernel, n_bm=len(bms)),
        grid_spec=pltpu.PrefetchScalarGridSpec(
            num_scalar_prefetch=1,
            grid=(groups // 2,),
            in_specs=[pair(v) for v in bms + mls],
            out_specs=pl.BlockSpec((1, 8, 128), lambda g, p: (g, 0, 0)),
            scratch_shapes=[pltpu.VMEM((GROUP * 4, 128, 128), F32)],
        ),
        out_shape=jax.ShapeDtypeStruct((groups // 2, 8, 128), F32),
        compiler_params=pltpu.CompilerParams(vmem_limit_bytes=VMEM),
        name="teacher",
    )(pos, *bms, *mls)


def packed(packs, si, x, at, n):
    crel, yrel = si // 2, si % 2
    return jnp.concatenate(
        [packs[crel * 4 + rz][(xx - x) & 3, yrel, pl.ds(at, n), :] for rz in range(4) for xx in range(4)],
        axis=0,
    )


def gate_kernel(pos_ref, *refs):
    packs = refs[:8]
    wq_ref, wk_ref, gate_ref, log_ref, xh_ref, xl_ref, kh_ref, kl_ref, qh_ref, ql_ref = refs[8:]
    z, x = pos_ref[0], pos_ref[1]
    gp = pl.program_id(0)
    for gg in range(2):
        g = gp * 2 + gg
        row = lax.broadcasted_iota(jnp.int32, (QB, CB), 0)
        col = lax.broadcasted_iota(jnp.int32, (QB, CB), 1)
        pick = (
            (col % 8 == g * 2 + row % 2)
            & (col // 16 % 4 == row // 8)
            & (col // 64 == ((row % 8 // 2 - z) & 3))
        )
        pick = jnp.where(pick, 1.0, 0.0).astype(BF16)
        ahead = ((col // 64 + z) & 3) * 64 + col % 64 - (row % 8 // 2 * 8 + row // 8 * 2 + row % 2)
        ahead = ahead.astype(F32)
        xs, qs = [[] for _ in range(GROUP)], []
        for si in range(4):
            ks = [packed(packs, si, x, pl.multiple_of(g * 64 + p * 16, 16), 16) for p in range(4)]
            proj_k = sum(mm(ks[p], wk_ref[gg, min(p, 2) * HD:(min(p, 2) + 1) * HD, :]) for p in range(4))
            raw = None
            for p in range(GROUP):
                rows = packed(packs, si, x, PQ_AT + p * 16, 16)
                part = mm(rows, wq_ref[gg, p * HD:(p + 1) * HD, :])
                raw = part if raw is None else raw + part
                xs[p].append(mm(pick, rows))
            raw = split2(raw)
            proj_q = mm(pick, raw[0]) + mm(pick, raw[1])
            qs.append(proj_q)
            proj_k2 = split2(proj_k)
            kh_ref[gg, si * CB:(si + 1) * CB, :] = proj_k2[0]
            kl_ref[gg, si * CB:(si + 1) * CB, :] = proj_k2[1]
            logits = mm3(split2(proj_q), proj_k2, NT) * SCALE
            start = packs[si // 2 * 4][0, si % 2, START_AT:START_AT + 16, :].astype(F32)[0:1, 0:1]
            live = ahead <= start
            masked = jnp.where(live, logits, NEG)
            top = masked.max(axis=1, keepdims=True)
            ex = jnp.where(live, jnp.exp(masked - top), 0.0)
            total = ex.sum(axis=1, keepdims=True)
            gate_ref[gg, si * QB:(si + 1) * QB, :] = ex / total
            log_ref[gg, si * QB:(si + 1) * QB, :] = jnp.where(live, masked - top - jnp.log(total), 0.0)
        for p in range(GROUP):
            hi, lo = split2(jnp.concatenate(xs[p], axis=0).T)
            xh_ref[gg, p * HD:(p + 1) * HD, :] = hi
            xl_ref[gg, p * HD:(p + 1) * HD, :] = lo
        hi, lo = split2(jnp.concatenate(qs, axis=0).T)
        qh_ref[gg] = hi
        ql_ref[gg] = lo


def gate_part(pos, packs, wq, wk):
    groups = wq.shape[0]
    whole = lambda v: pl.BlockSpec(v.shape, lambda g, p: (0,) * v.ndim)
    pair = lambda s: pl.BlockSpec((2,) + s[1:], lambda g, p: (g, 0, 0))
    seq_q, seq_k = 4 * QB, 4 * CB
    shapes = [(seq_q, CB)] * 2 + [(GROUP * HD, seq_q)] * 2 + [(seq_k, HD)] * 2 + [(HD, seq_q)] * 2
    shapes = [(groups,) + s for s in shapes]
    return pl.pallas_call(
        gate_kernel,
        grid_spec=pltpu.PrefetchScalarGridSpec(
            num_scalar_prefetch=1,
            grid=(groups // 2,),
            in_specs=[whole(v) for v in packs] + [pair(wq.shape), pair(wk.shape)],
            out_specs=[pair(s) for s in shapes],
        ),
        out_shape=[jax.ShapeDtypeStruct(s, F32 if i < 2 else BF16) for i, s in enumerate(shapes)],
        compiler_params=pltpu.CompilerParams(vmem_limit_bytes=VMEM),
        cost_estimate=pl.CostEstimate(flops=2 * 10 ** 9, bytes_accessed=10 ** 7, transcendentals=10 ** 6),
        name="gate",
    )(pos, *packs, wq, wk)


def grads_kernel(pos_ref, *refs):
    packs = refs[:8]
    t_ref, gate_ref, log_ref, xh_ref, xl_ref, kh_ref, kl_ref, qh_ref, ql_ref = refs[8:17]
    gq_ref, gk_ref, loss_ref = refs[17:]
    z, x, y, c = [pos_ref[i] for i in range(4)]
    gp = pl.program_id(0)
    for gg in range(2):
        g = gp * 2 + gg
        d_q, d_k = [], []
        for si in range(4):
            yy, cc = y ^ (si % 2), c ^ (si // 2)
            teacher = jnp.concatenate(
                [
                    jnp.concatenate(
                        [t_ref[(z + rz) & 3, xx, yy, cc, 0, :, gg * 64:gg * 64 + 64] for rz in range(4)], axis=1
                    )
                    for xx in range(4)
                ],
                axis=0,
            )
            target = teacher / teacher.sum(axis=1, keepdims=True)
            at = slice(si * QB, (si + 1) * QB)
            if si == 0:
                some = target > 0.0
                term = jnp.where(some, target * jnp.log(jnp.where(some, target, 1.0)), 0.0)
                term = term - target * log_ref[gg, at, :]
                loss = term.sum(axis=1, keepdims=True).sum(axis=0, keepdims=True) * (1.0 / QB)
                loss_ref[0, gg:gg + 1, :] = jnp.broadcast_to(loss, (1, 128))
            slope = split2((gate_ref[gg, at, :] - target) * (SCALE / QB))
            ks = slice(si * CB, (si + 1) * CB)
            d_q.append(mm3(slope, (kh_ref[gg, ks, :], kl_ref[gg, ks, :])))
            d_k.append(mm3((qh_ref[gg, :, at], ql_ref[gg, :, at]), slope))
        d_q = split2(jnp.concatenate(d_q, axis=0))
        gq_ref[gg] = mm3((xh_ref[gg], xl_ref[gg]), d_q)
        d_k = split2(jnp.concatenate(d_k, axis=1))
        for p in range(3):
            rows = [
                jnp.concatenate(
                    [packed(packs, si, x, pl.multiple_of(g * 64 + i * 16, 16), 16) for si in range(4)], axis=0
                )
                for i in ([p] if p < 2 else [2, 3])
            ]
            out = mm(d_k[0], rows[0]) + mm(d_k[1], rows[0])
            if p == 2:
                out = out + mm(d_k[0], rows[1])
            gk_ref[gg, p * HD:(p + 1) * HD, :] = out.T


def gradients(pos, packs, teachers, parts, wq, wk):
    groups = wq.shape[0]
    whole = lambda v: pl.BlockSpec(v.shape, lambda g, p: (0,) * v.ndim)
    pair = lambda v: pl.BlockSpec((2,) + v.shape[1:], lambda g, p: (g, 0, 0))
    return pl.pallas_call(
        grads_kernel,
        grid_spec=pltpu.PrefetchScalarGridSpec(
            num_scalar_prefetch=1,
            grid=(groups // 2,),
            in_specs=[whole(v) for v in packs]
            + [pl.BlockSpec((4, 4, 2, 2, 1, 8, 128), lambda g, p: (0, 0, 0, 0, g, 0, 0))]
            + [pair(v) for v in parts],
            out_specs=[pair(wq), pair(wk), pl.BlockSpec((1, 2, 128), lambda g, p: (g, 0, 0))],
        ),
        out_shape=[
            jax.ShapeDtypeStruct(wq.shape, F32),
            jax.ShapeDtypeStruct(wk.shape, F32),
            jax.ShapeDtypeStruct((groups // 2, 2, 128), F32),
        ],
        compiler_params=pltpu.CompilerParams(vmem_limit_bytes=VMEM),
        name="gradients",
    )(pos, *packs, teachers, *parts)


def shift(x, axis, by):
    return lax.ppermute(x, axis, [(i, (i + by) % 4) for i in range(4)])


def swap(x, axis):
    return lax.ppermute(x, axis, [(0, 1), (1, 0)])


def per_device(queries, keys, start_block, lengths, gate_query, gate_key):
    del lengths
    z, x = lax.axis_index("z"), lax.axis_index("x")
    y, c = lax.axis_index("y"), lax.axis_index("c")
    q, k = queries[0], keys[0]
    start = start_block[0]
    q_before, q_after = shift(q, "z", 1), shift(q, "z", -1)
    k_before, k_after = shift(k, "x", 1), shift(k, "x", -1)
    q_far = jnp.concatenate([shift(q_before[:64], "z", 1), shift(q_after[64:], "z", -1)], axis=0)
    k_far = [shift(k_before[:512], "x", 1), shift(k_after[512:], "x", -1)]
    pack = pool(start_block, q, k)
    pack = jnp.stack([pack, swap(pack, "y")])
    pack = jnp.stack([pack, shift(pack, "x", -1), shift(pack, "x", 2), shift(pack, "x", 1)])
    packs = [pack, shift(pack, "z", -1), shift(pack, "z", 2), shift(pack, "z", 1)]
    packs = packs + [swap(v, "c") for v in packs]
    ints = lambda *v: jnp.stack([jnp.asarray(i, jnp.int32) for i in v])
    offs = (0, 3, 1, 2)
    q_pos = [start + (((z + o) & 3) * 4 + x) * 2 for o in offs]
    k_pos = [(z * 4 + ((x + o) & 3)) * 16 for o in offs]
    bm1, ml1, qs1 = block_scores(ints(*q_pos[:3], k_pos[0]), [q, q_before, q_after], [k])
    bm2, ml2, qs2 = block_scores(ints(q_pos[3], k_pos[0]), [q_far], [k])
    bm3, ml3 = block_scores(ints(*q_pos, *k_pos[1:3]), [qs1, qs2], [k_before, k_after], [ml1, ml2])
    at = [(z + o) & 3 for o in offs]
    bm4, ml4 = block_scores(
        ints(*q_pos, k_pos[3], k_pos[3] + 8, *at), [qs1, qs2], k_far, [ml3], place=True
    )
    place = ints(z, x, y, c)
    mls = [ml4, shift(ml4, "z", 1), shift(ml4, "z", -1), shift(ml4, "z", 2)]
    place_late, packs, _ = lax.optimization_barrier((place, packs, ml4))
    parts = gate_part(place_late, packs, gate_query, gate_key)
    teacher = teacher_blocks(place, [bm1, bm2, bm3, bm4], mls)
    teachers = lax.all_to_all(
        jnp.broadcast_to(teacher[None], (64,) + teacher.shape), ("z", "x", "y", "c"), 0, 0, tiled=True
    ).reshape((4, 4, 2, 2) + teacher.shape)
    grad_q, grad_k, loss = gradients(place, packs, teachers, parts, gate_query, gate_key)
    return grad_q, grad_k, loss[:, :, 0].reshape(1, 4)


def solution(mesh):
    fine = Mesh(mesh.devices.reshape(4, 4, 2, 2, 2), ("z", "x", "h", "y", "c"))
    ctx, dp = ("z", "x"), ("y", "c")
    placed = (
        P(dp, ctx, "h"),
        P(dp, ctx, "h"),
        P(dp),
        P(dp),
        P("h", None, None),
        P("h", None, None),
    )
    return jax.shard_map(
        per_device,
        mesh=fine,
        in_specs=placed,
        out_specs=(P("h", None, None), P("h", None, None), P(dp, "h")),
        check_vma=False,
    )
```

```python
import functools
import math

import jax
import jax.numpy as jnp
from jax import lax
from jax.experimental import pallas as pl
from jax.experimental.pallas import tpu as pltpu
from jax.sharding import Mesh, PartitionSpec as P

BLK = 64
GROUP = 5
HD = 128
QB = 32
CB = 256
NEG = -1e30
FLOOR = -1e20
KT = 512
KB = KT // BLK
SAFE = 100.0
SCALE = HD ** -0.5
SCALE2 = SCALE * math.log2(math.e)
VMEM = 56 * 2 ** 20
F32 = jnp.float32
BF16 = jnp.bfloat16
NT = (((1,), (1,)), ((), ()))
TN = (((0,), (0,)), ((), ()))
NN = (((1,), (0,)), ((), ()))
PQ_AT = 256
START_AT = PQ_AT + 80
PACK = START_AT + 16


def split2(x):
    hi = x.astype(BF16)
    return hi, (x - hi.astype(F32)).astype(BF16)


def mm(a, b, dims=NN):
    return lax.dot_general(a, b, dims, preferred_element_type=F32)


def mm3(a, b, dims=NN):
    return mm(a[0], b[0], dims) + (mm(a[0], b[1], dims) + mm(a[1], b[0], dims))


def block_tops(s):
    return s.reshape(s.shape[0] // BLK, 8, 8, s.shape[1]).max(axis=1).max(axis=1)


def part_sums(s, m):
    return jnp.exp2(s - m).reshape(s.shape[0] // 8, 8, s.shape[1]).sum(axis=0)


def scores_kernel(pos_ref, *refs, q_rows, k_rows):
    nq, nk = len(q_rows), len(k_rows)
    q_refs, k_refs = refs[:nq], refs[nq:nq + nk]
    bm_ref, ml_ref, qs, ks, d_s, bad_s = refs[nq + nk:]
    rt, kn = sum(q_rows), sum(k_rows)
    q_pos = [pos_ref[i] for i in range(4)]
    kp = [pos_ref[4 + i] for i in range(4)]
    for i, (r, n) in enumerate(zip(q_refs, q_rows)):
        at = pl.multiple_of(pos_ref[8 + i], BLK)
        for h in range(GROUP):
            hi, lo = split2(r[:, h * HD:(h + 1) * HD].astype(F32) * SCALE2)
            qs[h, pl.ds(at, n), :] = jnp.concatenate([hi, lo], axis=1)
    for i, (r, n) in enumerate(zip(k_refs, k_rows)):
        ks[pl.ds(pl.multiple_of(pos_ref[8 + nq + i], KT), n), :] = r[...]
    tiles = range(kn // KT)
    piece = kn // 4
    low, high = functools.reduce(jnp.minimum, q_pos), functools.reduce(jnp.maximum, q_pos)
    fulls = [k + piece // BLK - 1 < low for k in kp]
    full = fulls[0] & fulls[1] & fulls[2] & fulls[3]
    half = fulls[0] & fulls[1] & jnp.logical_not(full)
    none = functools.reduce(jnp.minimum, kp) > high + 1
    rest = jnp.logical_not(full | half | none)

    def scores(t, h):
        k = ks[t * KT:(t + 1) * KT, :]
        return mm(jnp.concatenate([k, k], axis=1), qs[h], NT)

    def seen(p):
        lane = lax.broadcasted_iota(jnp.int32, (8, rt), 1)
        d = lane % 128 - lax.broadcasted_iota(jnp.int32, (8, rt), 0)
        for i, v in enumerate(q_pos):
            d = d + jnp.where(lane // 128 == i, (v - kp[p]) * BLK, 0)
        return d

    def masked(t, h):
        p, o = t * KT // piece, t * KT % piece
        keep = jnp.concatenate([d_s[p] >= o + i for i in range(0, KT, 8)], axis=0)
        return jnp.where(keep, scores(t, h), NEG)

    def store(h, m, l):
        ml_ref[0, h, 0:1, :] = m
        ml_ref[0, h, 1:2, :] = l.sum(axis=0, keepdims=True)

    def heads(from_piece):
        for p in range(from_piece, 4):
            d_s[p] = seen(p)

        def head(h, worst):
            found = []
            for t in tiles:
                p, first = t * KT // piece, t * KT % piece == 0
                s = masked(t, h) if p >= from_piece else scores(t, h)
                if t == 0 or (first and p >= from_piece):
                    m = s[:BLK].reshape(8, 8, rt).max(axis=0).max(axis=0, keepdims=True)
                    if p >= from_piece:
                        m = jnp.maximum(m, FLOOR)
                    found.append([m, m, None])
                top, part = block_tops(s), part_sums(s, m)
                bm_ref[0, h, t * KB:(t + 1) * KB, :] = top
                f = found[-1]
                f[1] = jnp.maximum(f[1], top.max(axis=0, keepdims=True))
                f[2] = part if f[2] is None else f[2] + part
            big = functools.reduce(jnp.maximum, [f[1] for f in found])
            store(h, big, sum(f[2] * jnp.exp2(f[0] - big) for f in found))
            return functools.reduce(jnp.maximum, [f[1] - f[0] for f in found], worst)

        bad_s[0] = jnp.max(lax.fori_loop(0, GROUP, head, jnp.zeros((1, rt), F32)))

    pl.when(full)(lambda: heads(4))
    pl.when(half)(lambda: heads(2))
    pl.when(rest)(lambda: heads(0))

    @pl.when(none)
    def _():
        bm_ref[...] = jnp.full(bm_ref.shape, NEG, F32)
        ml_ref[0, :, 0:1, :] = jnp.full((GROUP, 1, rt), FLOOR, F32)
        ml_ref[0, :, 1:2, :] = jnp.zeros((GROUP, 1, rt), F32)
        bad_s[0] = 0.0

    @pl.when(bad_s[0] > SAFE)
    def _():
        for p in range(4):
            d_s[p] = seen(p)

        def head(h, _):
            m, l = jnp.full((1, rt), FLOOR, F32), jnp.zeros((8, rt), F32)
            for t in tiles:
                s = masked(t, h)
                top = block_tops(s)
                bm_ref[0, h, t * KB:(t + 1) * KB, :] = top
                new = jnp.maximum(m, top.max(axis=0, keepdims=True))
                l = l * jnp.exp2(m - new) + part_sums(s, new)
                m = new
            store(h, m, l)
            return 0

        lax.fori_loop(0, GROUP, head, 0)


def block_scores(pos, q_parts, k_parts, first):
    q_rows = [q.shape[0] for q in q_parts]
    k_rows = [k.shape[0] for k in k_parts]
    rt, kn = sum(q_rows), sum(k_rows)
    spec = lambda v, w: pl.BlockSpec(
        (v.shape[0], w), functools.partial(lambda o, g, p: (0, o + g), first if v.shape[1] > 2 * w else 0)
    )
    shapes = [(2, GROUP, kn // BLK, rt), (2, GROUP, 2, rt)]
    return pl.pallas_call(
        functools.partial(scores_kernel, q_rows=q_rows, k_rows=k_rows),
        grid_spec=pltpu.PrefetchScalarGridSpec(
            num_scalar_prefetch=1,
            grid=(2,),
            in_specs=[spec(q, GROUP * HD) for q in q_parts] + [spec(k, HD) for k in k_parts],
            out_specs=[pl.BlockSpec((1,) + s[1:], lambda g, p: (g, 0, 0, 0)) for s in shapes],
            scratch_shapes=[
                pltpu.VMEM((GROUP, rt, 2 * HD), BF16),
                pltpu.VMEM((kn, HD), BF16),
                pltpu.VMEM((4, 8, rt), jnp.int32),
                pltpu.SMEM((1,), F32),
            ],
        ),
        out_shape=[jax.ShapeDtypeStruct(s, F32) for s in shapes],
        compiler_params=pltpu.CompilerParams(vmem_limit_bytes=VMEM),
        name="block_scores",
    )(pos, *q_parts, *k_parts)


def pool_kernel(start_ref, q_ref, k_ref, out_ref):
    groups = k_ref.shape[1] // HD
    for g in range(groups):
        x = k_ref[:, g * HD:(g + 1) * HD].astype(F32).reshape(16, BLK, HD)
        hi, lo = split2(x.sum(axis=1) * (1.0 / BLK))
        parts = [x.max(axis=1).astype(BF16), x.min(axis=1).astype(BF16), hi, lo]
        for p, part in enumerate(parts):
            out_ref[g * 64 + p * 16:g * 64 + p * 16 + 16, :] = part
    for p in range(GROUP):
        rows = []
        for g in range(groups):
            at = (g * GROUP + p) * HD
            x = q_ref[:, at:at + HD].astype(F32).reshape(2, BLK, HD)
            rows.append(x.sum(axis=1) * (1.0 / BLK))
        hi, lo = split2(jnp.concatenate(rows, axis=0))
        at = PQ_AT + p * 16
        out_ref[at:at + 16, :] = jnp.concatenate([hi.astype(F32), lo.astype(F32)], axis=0).astype(BF16)
    out_ref[START_AT:, :] = jnp.full((16, HD), start_ref[0].astype(F32), F32).astype(BF16)


def pool(start_block, q, k):
    return pl.pallas_call(
        pool_kernel,
        in_specs=[
            pl.BlockSpec(memory_space=pltpu.SMEM),
            pl.BlockSpec(memory_space=pltpu.VMEM),
            pl.BlockSpec(memory_space=pltpu.VMEM),
        ],
        out_specs=pl.BlockSpec(memory_space=pltpu.VMEM),
        out_shape=jax.ShapeDtypeStruct((PACK, HD), BF16),
        compiler_params=pltpu.CompilerParams(vmem_limit_bytes=VMEM),
        name="pool",
    )(start_block, q, k)


def teacher_kernel(*refs):
    bm_refs, ml_refs, out_ref = refs[:2], refs[2:-1], refs[-1]
    for gp in range(2):
        totals = [None] * 4
        for h in range(GROUP):
            xs = []
            for gg in range(2):
                g = gp * 2 + gg
                ms = [m[g, h, 0:1, :] for m in ml_refs]
                m = functools.reduce(jnp.maximum, ms)
                l = sum(ref[g, h, 1:2, :] * jnp.exp2(mi - m) for ref, mi in zip(ml_refs, ms))
                xs.append(bm_refs[gp][gg, h] - (m + jnp.log(l) * math.log2(math.e)))
            for i in range(4):
                t = jnp.concatenate([v[:, i * 128:(i + 1) * 128] for v in xs], axis=0).T
                top = jnp.exp2(t.reshape(2, BLK, 128).max(axis=1))
                totals[i] = top if h == 0 else totals[i] + top
        tile = jnp.concatenate(totals, axis=0) * (1.0 / GROUP)
        out_ref[:, gp] = jnp.broadcast_to(tile[None], (out_ref.shape[0],) + tile.shape)


def teacher_blocks(bms, mls, copies):
    return pl.pallas_call(
        teacher_kernel,
        in_specs=[pl.BlockSpec(memory_space=pltpu.VMEM)] * (len(bms) + len(mls)),
        out_specs=pl.BlockSpec(memory_space=pltpu.VMEM),
        out_shape=jax.ShapeDtypeStruct((copies, 2, 8, 128), F32),
        compiler_params=pltpu.CompilerParams(vmem_limit_bytes=VMEM),
        name="teacher",
    )(*bms, *mls)


def packed(pack_ref, si, at):
    return pack_ref[:, :, si, pl.ds(at, 16), :].reshape(CB, HD)


def gate_kernel(pack_ref, wq_ref, wk_ref, gate_ref, log_ref, xh_ref, xl_ref, kh_ref, kl_ref, qh_ref, ql_ref):
    gp = pl.program_id(0)
    row = lax.broadcasted_iota(jnp.int32, (2 * QB, CB), 0)
    col = lax.broadcasted_iota(jnp.int32, (2 * QB, CB), 1)
    a = row % QB
    pick = (
        (col % 8 == (gp * 2 + row // QB) * 2 + a % 2)
        & (col // 16 % 4 == a // 8)
        & (col // 64 == a % 8 // 2)
    )
    pick = jnp.where(pick, 1.0, 0.0).astype(BF16)
    a = a[:QB]
    ahead = (col[:QB] - (a % 8 // 2 * 8 + a // 8 * 2 + a % 2)).astype(F32)
    wq = jnp.concatenate([wq_ref[0], wq_ref[1]], axis=1)
    xs, qs = [[], []], [[], []]
    for si in range(2):
        rows = jnp.concatenate([packed(pack_ref, si, PQ_AT + p * 16) for p in range(GROUP)], axis=1)
        raw = split2(mm(rows, wq))
        both = mm(pick, rows)
        start = pack_ref[0, 0, si, START_AT:START_AT + 16, :].astype(F32)[0:1, 0:1]
        live = ahead <= start
        for gg in range(2):
            g = gp * 2 + gg
            ks = [packed(pack_ref, si, pl.multiple_of(g * 64 + p * 16, 16)) for p in range(4)]
            mean = wk_ref[gg, 2 * HD:, :]
            proj_k = mm(jnp.concatenate(ks[:2], axis=1), wk_ref[gg, :2 * HD, :])
            proj_k = proj_k + mm(jnp.concatenate(ks[2:], axis=1), jnp.concatenate([mean, mean], axis=0))
            xs[gg].append(both[gg * QB:(gg + 1) * QB])
            mine, lanes = pick[gg * QB:(gg + 1) * QB], slice(gg * HD, (gg + 1) * HD)
            proj_q = mm(mine, raw[0][:, lanes]) + mm(mine, raw[1][:, lanes])
            qs[gg].append(proj_q)
            proj_k = split2(proj_k)
            kh_ref[gg, si * CB:(si + 1) * CB, :] = proj_k[0]
            kl_ref[gg, si * CB:(si + 1) * CB, :] = proj_k[1]
            logits = mm3(split2(proj_q), proj_k, NT) * SCALE
            masked = jnp.where(live, logits, NEG)
            top = masked.max(axis=1, keepdims=True)
            ex = jnp.where(live, jnp.exp(masked - top), 0.0)
            total = ex.sum(axis=1, keepdims=True)
            gate_ref[gg, si * QB:(si + 1) * QB, :] = ex / total
            if si == 0:
                log_ref[gg] = jnp.where(live, masked - top - jnp.log(total), 0.0)
    for gg in range(2):
        hi, lo = split2(jnp.concatenate(xs[gg], axis=0).T)
        xh_ref[gg] = hi
        xl_ref[gg] = lo
        hi, lo = split2(jnp.concatenate(qs[gg], axis=0).T)
        qh_ref[gg] = hi
        ql_ref[gg] = lo


def pair_spec(shape):
    return pl.BlockSpec((2,) + tuple(shape[1:]), lambda g: (g,) + (0,) * (len(shape) - 1))


def whole_spec(shape):
    return pl.BlockSpec(tuple(shape), lambda g: (0,) * len(shape))


def gate_part(pack, wq, wk):
    shapes = [(2 * QB, CB), (QB, CB)] + [(GROUP * HD, 2 * QB)] * 2 + [(2 * CB, HD)] * 2 + [(HD, 2 * QB)] * 2
    shapes = [(4,) + s for s in shapes]
    return pl.pallas_call(
        gate_kernel,
        grid=(2,),
        in_specs=[whole_spec(pack.shape), pair_spec(wq.shape), pair_spec(wk.shape)],
        out_specs=[pair_spec(s) for s in shapes],
        out_shape=[jax.ShapeDtypeStruct(s, F32 if i < 2 else BF16) for i, s in enumerate(shapes)],
        compiler_params=pltpu.CompilerParams(vmem_limit_bytes=VMEM),
        cost_estimate=pl.CostEstimate(flops=10 ** 10, bytes_accessed=10 ** 7, transcendentals=10 ** 6),
        name="gate",
    )(pack, wq, wk)


def grads_kernel(y_ref, pack_ref, t_ref, gate_ref, log_ref, xh_ref, xl_ref, kh_ref, kl_ref, qh_ref, ql_ref, g_ref, loss_ref):
    gp = pl.program_id(0)
    wide = GROUP * HD
    for gg in range(2):
        g = gp * 2 + gg
        d_q, d_k = [], []
        for si in range(2):
            yy = y_ref[0] ^ si
            teacher = jnp.concatenate(
                [
                    jnp.concatenate([t_ref[z, x, yy, 0, :, gg * 64:gg * 64 + 64] for z in range(4)], axis=1)
                    for x in range(4)
                ],
                axis=0,
            )
            target = teacher / teacher.sum(axis=1, keepdims=True)
            at = slice(si * QB, (si + 1) * QB)
            if si == 0:
                some = target > 0.0
                term = jnp.where(some, target * jnp.log(jnp.where(some, target, 1.0)), 0.0)
                term = term - target * log_ref[gg]
                loss = term.sum(axis=1, keepdims=True).sum(axis=0, keepdims=True) * (1.0 / QB)
                loss_ref[0, gg:gg + 1, :] = jnp.broadcast_to(loss, (1, 128))
            slope = split2((gate_ref[gg, at, :] - target) * (SCALE / QB))
            ks = slice(si * CB, (si + 1) * CB)
            d_q.append(mm3(slope, (kh_ref[gg, ks, :], kl_ref[gg, ks, :])))
            d_k.append(mm3((qh_ref[gg, :, at], ql_ref[gg, :, at]), slope))
        d_q = split2(jnp.concatenate(d_q, axis=0))
        g_ref[gg, :wide, :] = mm3((xh_ref[gg], xl_ref[gg]), d_q)
        d_k = jnp.concatenate(split2(jnp.concatenate(d_k, axis=1)), axis=0)
        rows = [
            jnp.concatenate([packed(pack_ref, si, pl.multiple_of(g * 64 + p * 16, 16)) for si in range(2)], axis=0)
            for p in range(4)
        ]
        ends = mm(d_k, jnp.concatenate(rows[:2], axis=1))
        mean = mm(d_k, jnp.concatenate(rows[2:], axis=1))
        ends = ends[:HD] + ends[HD:]
        mean = mean[:HD, :HD] + (mean[HD:, :HD] + mean[:HD, HD:])
        g_ref[gg, wide:wide + HD, :] = ends[:, :HD].T
        g_ref[gg, wide + HD:wide + 2 * HD, :] = ends[:, HD:].T
        g_ref[gg, wide + 2 * HD:, :] = mean.T


def gradients(y, pack, teachers, parts):
    out = (4, (GROUP + 3) * HD, HD)
    return pl.pallas_call(
        grads_kernel,
        grid=(2,),
        in_specs=[
            pl.BlockSpec(memory_space=pltpu.SMEM),
            whole_spec(pack.shape),
            pl.BlockSpec((4, 4, 2, 1, 8, 128), lambda g: (0, 0, 0, g, 0, 0)),
        ]
        + [pair_spec(v.shape) for v in parts],
        out_specs=[pair_spec(out), pl.BlockSpec((1, 2, 128), lambda g: (g, 0, 0))],
        out_shape=[jax.ShapeDtypeStruct(out, F32), jax.ShapeDtypeStruct((2, 2, 128), F32)],
        compiler_params=pltpu.CompilerParams(vmem_limit_bytes=VMEM),
        name="gradients",
    )(y, pack, teachers, *parts)


def shift(x, axis, by):
    return lax.ppermute(x, axis, [(i, (i + by) % 4) for i in range(4)])


def swap(x, axis):
    return lax.ppermute(x, axis, [(0, 1), (1, 0)])


def per_device(queries, keys, start_block, lengths, gate_query, gate_key):
    del lengths
    z, x, y = lax.axis_index("z"), lax.axis_index("x"), lax.axis_index("y")
    q, k = queries[0], keys[0]
    start = start_block[0]
    k0, k1 = k[:, :2 * HD], k[:, 2 * HD:]
    q_before, q_after = shift(q, "z", 1), shift(q, "z", -1)
    k0_before, k0_after = shift(k0, "x", 1), shift(k0, "x", -1)
    q_far = [shift(q_before[:64], "z", 1), shift(q_after[64:], "z", -1)]
    k0_far = [shift(k0_before[:512], "x", 1), shift(k0_after[512:], "x", -1)]
    q_own, k_own, *_ = lax.optimization_barrier((q, k, q_before, q_after, k0_before, k0_after))
    pack = pool(start_block, q_own, k_own)
    pack = jnp.stack([pack, swap(pack, "y")])
    pack = lax.all_gather(pack, ("z", "x")).reshape(4, 4, 2, PACK, HD)
    k1_parts = [shift(k1, "x", 1), shift(k1, "x", -1), shift(k1, "x", 2)]
    offs = (0, 3, 1, 2)
    zs, xs = [(z + o) & 3 for o in offs], [(x + o) & 3 for o in offs]
    q_pos = [start + (i * 4 + x) * 2 for i in range(4)]
    k_pos = [(z * 4 + i) * 16 for i in range(4)]
    q_at = [zs[0] * 128, zs[1] * 128, zs[2] * 128, zs[3] * 128, zs[3] * 128 + 64]
    k_at = [i * 1024 for i in xs]
    ints = lambda *v: jnp.stack([jnp.asarray(i, jnp.int32) for i in v])
    q_parts = [q, q_before, q_after] + q_far
    pos = ints(*q_pos, *k_pos, *q_at, *k_at, k_at[3] + 512)
    bm0, ml0 = block_scores(pos, q_parts, [k, k0_before, k0_after] + k0_far, 0)
    bm1, ml1 = block_scores(pos, q_parts, [k] + k1_parts, 2)
    ml = jnp.concatenate([ml0, ml1], axis=0)
    mls = [ml, shift(ml, "z", 1), shift(ml, "z", -1), shift(ml, "z", 2)]
    pack, _ = lax.optimization_barrier((pack, ml))
    parts = gate_part(pack, gate_query, gate_key)
    parts, mls = lax.optimization_barrier((parts, mls))
    teachers = teacher_blocks([bm0, bm1], mls, 32)
    teachers = lax.all_to_all(teachers, ("z", "x", "y"), 0, 0, tiled=True).reshape(4, 4, 2, 2, 8, 128)
    grads, loss = gradients(y.astype(jnp.int32).reshape(1), pack, teachers, parts)
    other = swap(grads, "c")
    wide = GROUP * HD
    grad_q = grads[:, :wide] + other[:, :wide]
    grad_k = grads[:, wide:] + other[:, wide:]
    return grad_q, grad_k, loss[:, :, 0].reshape(1, 4)


def solution(mesh):
    fine = Mesh(mesh.devices.reshape(4, 4, 2, 2, 2), ("z", "x", "h", "y", "c"))
    ctx, dp = ("z", "x"), ("y", "c")
    placed = (
        P(dp, ctx, "h"),
        P(dp, ctx, "h"),
        P(dp),
        P(dp),
        P("h", None, None),
        P("h", None, None),
    )
    return jax.shard_map(
        per_device,
        mesh=fine,
        in_specs=placed,
        out_specs=(P("h", None, None), P("h", None, None), P(dp, "h")),
        check_vma=False,
    )
```

```python
import functools
import itertools
import math

import jax
import jax.numpy as jnp
from jax import lax
from jax.experimental import pallas as pl
from jax.experimental.pallas import tpu as pltpu
from jax.sharding import Mesh, PartitionSpec as P

BLK = 64
GROUP = 5
HD = 128
QB = 32
CB = 256
NEG = -1e30
FLOOR = -1e20
KT = 512
KB = KT // BLK
SAFE = 100.0
SCALE = HD ** -0.5
SCALE2 = SCALE * math.log2(math.e)
VMEM = 56 * 2 ** 20
F32 = jnp.float32
BF16 = jnp.bfloat16
NT = (((1,), (1,)), ((), ()))
TN = (((0,), (0,)), ((), ()))
NN = (((1,), (0,)), ((), ()))
PQ_AT = 256
START_AT = PQ_AT + 80
PACK = START_AT + 16


def split2(x):
    hi = x.astype(BF16)
    return hi, (x - hi.astype(F32)).astype(BF16)


def mm(a, b, dims=NN):
    return lax.dot_general(a, b, dims, preferred_element_type=F32)


def mm3(a, b, dims=NN):
    return mm(a[0], b[0], dims) + (mm(a[0], b[1], dims) + mm(a[1], b[0], dims))


def block_tops(s):
    return s.reshape(s.shape[0] // BLK, 8, 8, s.shape[1]).max(axis=1).max(axis=1)


def part_sums(s, m):
    return jnp.exp2(s - m).reshape(s.shape[0] // 8, 8, s.shape[1]).sum(axis=0)


def scores_kernel(pos_ref, *refs, n_q, nk):
    refs = list(refs)
    take = lambda n: [refs.pop(0) for _ in range(n)]
    q_refs, k_refs = take(n_q), take(nk)
    first = n_q > 1
    ml_in = [] if first else take(1)
    bm_ref, ml_ref = take(2)
    qs = take(1)[0] if first else q_refs[0]
    d_s, bad_s = refs
    rt, piece = qs.shape[2], k_refs[0].shape[0]
    q_pos = [pos_ref[i] for i in range(4)]
    kp = [pos_ref[4 + i] for i in range(nk)]
    if first:
        for i, r in enumerate(q_refs):
            at = pl.multiple_of(pos_ref[4 + nk + i], 128)
            for h in range(GROUP):
                hi, lo = split2(r[:, h * HD:(h + 1) * HD].astype(F32) * SCALE2)
                qs[0, h, pl.ds(at, 128), :] = jnp.concatenate([hi, lo], axis=1)
    tiles = [(p, o) for p in range(nk) for o in range(0, piece, KT)]
    low, high = functools.reduce(jnp.minimum, q_pos), functools.reduce(jnp.maximum, q_pos)
    full = [k + piece // BLK - 1 < low for k in kp]
    none = functools.reduce(jnp.minimum, kp) > high + 1

    def scores(t, h):
        p, o = tiles[t]
        k = k_refs[p][o:o + KT, :]
        return mm(jnp.concatenate([k, k], axis=1), qs[0, h], NT)

    def seen(p):
        lane = lax.broadcasted_iota(jnp.int32, (8, rt), 1)
        d = lane % 128 - lax.broadcasted_iota(jnp.int32, (8, rt), 0)
        for i, v in enumerate(q_pos):
            d = d + jnp.where(lane // 128 == i, (v - kp[p]) * BLK, 0)
        return d

    def masked(t, h):
        p, o = tiles[t]
        keep = jnp.concatenate([d_s[p] >= o + i for i in range(0, KT, 8)], axis=0)
        return jnp.where(keep, scores(t, h), NEG)

    def store(h, found):
        if ml_in:
            m = ml_in[0][0, h, 0:1, :]
            found = found + [(m, m, ml_in[0][0, h, 1:2, :])]
        big = functools.reduce(jnp.maximum, [f[1] for f in found])
        ml_ref[0, h, 0:1, :] = big
        ml_ref[0, h, 1:2, :] = sum(f[2] * jnp.exp2(f[0] - big) for f in found)

    def heads(masks):
        for p in range(nk):
            if masks[p]:
                d_s[p] = seen(p)
        worst = jnp.zeros((1, rt), F32)
        for h in range(GROUP):
            found = []
            for t, (p, o) in enumerate(tiles):
                s = masked(t, h) if masks[p] else scores(t, h)
                if t == 0 or (o == 0 and (masks[p] or masks[p - 1])):
                    m = s[:BLK].reshape(8, 8, rt).max(axis=0).max(axis=0, keepdims=True)
                    m = jnp.maximum(m, FLOOR) if masks[p] else m
                    found.append([m, m, None])
                top, part = block_tops(s), part_sums(s, m)
                bm_ref[0, h, t * KB:(t + 1) * KB, :] = top
                f = found[-1]
                f[1] = jnp.maximum(f[1], top.max(axis=0, keepdims=True))
                f[2] = part if f[2] is None else f[2] + part
            worst = functools.reduce(jnp.maximum, [f[1] - f[0] for f in found], worst)
            store(h, [(f[0], f[1], f[2].sum(axis=0, keepdims=True)) for f in found])
        bad_s[0] = jnp.max(worst)

    for masks in itertools.product((False, True), repeat=nk):
        match = functools.reduce(jnp.logical_and, [f != m for f, m in zip(full, masks)])
        pl.when(match & jnp.logical_not(none))(functools.partial(heads, masks))

    @pl.when(none)
    def _():
        bm_ref[...] = jnp.full(bm_ref.shape, NEG, F32)
        for h in range(GROUP):
            store(h, [(jnp.full((1, rt), FLOOR, F32), jnp.full((1, rt), FLOOR, F32), jnp.zeros((1, rt), F32))])
        bad_s[0] = 0.0

    @pl.when(bad_s[0] > SAFE)
    def _():
        for p in range(nk):
            d_s[p] = seen(p)

        def head(h, _):
            m, l = jnp.full((1, rt), FLOOR, F32), jnp.zeros((8, rt), F32)
            for t in range(len(tiles)):
                s = masked(t, h)
                top = block_tops(s)
                bm_ref[0, h, t * KB:(t + 1) * KB, :] = top
                new = jnp.maximum(m, top.max(axis=0, keepdims=True))
                l = l * jnp.exp2(m - new) + part_sums(s, new)
                m = new
            store(h, [(m, m, l.sum(axis=0, keepdims=True))])
            return 0

        lax.fori_loop(0, GROUP, head, 0)


def block_scores(pos, q_parts, k_parts, ml_in=()):
    first = len(q_parts) > 1
    rt, kn = 512, sum(k.shape[0] for k in k_parts)
    groups = k_parts[0].shape[1] // HD
    per_group = lambda s: pl.BlockSpec((1,) + tuple(s[1:]), lambda g, p: (g, 0, 0, 0))
    lanes = lambda v: pl.BlockSpec((v.shape[0], v.shape[1] // groups), lambda g, p: (0, g))
    shapes = [(groups, GROUP, kn // BLK, rt), (groups, GROUP, 2, rt)] + [(groups, GROUP, rt, 2 * HD)] * first
    return pl.pallas_call(
        functools.partial(scores_kernel, n_q=len(q_parts), nk=len(k_parts)),
        grid_spec=pltpu.PrefetchScalarGridSpec(
            num_scalar_prefetch=1,
            grid=(groups,),
            in_specs=[lanes(q) if first else per_group(q.shape) for q in q_parts]
            + [lanes(k) for k in k_parts]
            + [per_group(m.shape) for m in ml_in],
            out_specs=[per_group(s) for s in shapes],
            scratch_shapes=[pltpu.VMEM((len(k_parts), 8, rt), jnp.int32), pltpu.SMEM((1,), F32)],
        ),
        out_shape=[jax.ShapeDtypeStruct(s, t) for s, t in zip(shapes, (F32, F32, BF16))],
        compiler_params=pltpu.CompilerParams(vmem_limit_bytes=VMEM),
        name="block_scores",
    )(pos, *q_parts, *k_parts, *ml_in)


def pool_kernel(start_ref, q_ref, k_ref, out_ref):
    groups = k_ref.shape[1] // HD
    for g in range(groups):
        x = k_ref[:, g * HD:(g + 1) * HD].astype(F32).reshape(16, BLK, HD)
        hi, lo = split2(x.sum(axis=1) * (1.0 / BLK))
        parts = [x.max(axis=1).astype(BF16), x.min(axis=1).astype(BF16), hi, lo]
        for p, part in enumerate(parts):
            out_ref[g * 64 + p * 16:g * 64 + p * 16 + 16, :] = part
    for p in range(GROUP):
        rows = []
        for g in range(groups):
            at = (g * GROUP + p) * HD
            x = q_ref[:, at:at + HD].astype(F32).reshape(2, BLK, HD)
            rows.append(x.sum(axis=1) * (1.0 / BLK))
        hi, lo = split2(jnp.concatenate(rows, axis=0))
        at = PQ_AT + p * 16
        out_ref[at:at + 16, :] = jnp.concatenate([hi.astype(F32), lo.astype(F32)], axis=0).astype(BF16)
    out_ref[START_AT:, :] = jnp.full((16, HD), start_ref[0].astype(F32), F32).astype(BF16)


def pool(start_block, q, k):
    return pl.pallas_call(
        pool_kernel,
        in_specs=[
            pl.BlockSpec(memory_space=pltpu.SMEM),
            pl.BlockSpec(memory_space=pltpu.VMEM),
            pl.BlockSpec(memory_space=pltpu.VMEM),
        ],
        out_specs=pl.BlockSpec(memory_space=pltpu.VMEM),
        out_shape=jax.ShapeDtypeStruct((PACK, HD), BF16),
        compiler_params=pltpu.CompilerParams(vmem_limit_bytes=VMEM),
        name="pool",
    )(start_block, q, k)


def teacher_kernel(x_ref, *refs):
    near, sides, far = refs[:3]
    ml_refs, (out_ref, sc) = refs[3:-2], refs[-2:]
    rt = near.shape[3]
    to = [pl.multiple_of(((x_ref[0] + o) & 3) * 16, 16) for o in (0, 3, 1, 2)]
    for g in range(4):
        for h in range(GROUP):
            ms = [m[g, h, 0:1, :] for m in ml_refs]
            m = functools.reduce(jnp.maximum, ms)
            l = sum(ref[g, h, 1:2, :] * jnp.exp2(mi - m) for ref, mi in zip(ml_refs, ms))
            lse = m + jnp.log(l) * math.log2(math.e)
            parts = [near[g, h], sides[g, h, :16], sides[g, h, 16:], far[g, h]]
            for at, v in zip(to, parts):
                sc[g // 2 * GROUP + h, pl.ds(at + g % 2 * 64, 16), :] = v - lse
    for gp in range(2):
        totals = [None] * (rt // 128)
        for h in range(GROUP):
            for i in range(rt // 128):
                t = sc[gp * GROUP + h, :, i * 128:(i + 1) * 128].T
                top = jnp.exp2(t.reshape(2, BLK, 128).max(axis=1))
                totals[i] = top if h == 0 else totals[i] + top
        tile = jnp.concatenate(totals, axis=0) * (1.0 / GROUP)
        out_ref[:, gp] = jnp.broadcast_to(tile[None], (out_ref.shape[0],) + tile.shape)


def teacher_blocks(x, bms, mls, copies):
    return pl.pallas_call(
        teacher_kernel,
        in_specs=[pl.BlockSpec(memory_space=pltpu.SMEM)]
        + [pl.BlockSpec(memory_space=pltpu.VMEM)] * (len(bms) + len(mls)),
        out_specs=pl.BlockSpec(memory_space=pltpu.VMEM),
        out_shape=jax.ShapeDtypeStruct((copies, 2, 8, 128), F32),
        scratch_shapes=[pltpu.VMEM((2 * GROUP, 128, bms[0].shape[3]), F32)],
        compiler_params=pltpu.CompilerParams(vmem_limit_bytes=VMEM),
        name="teacher",
    )(x, *bms, *mls)


def packed(pack_ref, si, at):
    return pack_ref[:, :, si, pl.ds(at, 16), :].reshape(CB, HD)


def gate_kernel(at_ref, *refs):
    parts, (wq_ref, wk_ref) = refs[:4], refs[4:6]
    pack_ref, gate_ref, log_ref, xh_ref, xl_ref, kh_ref, kl_ref, qh_ref, ql_ref = refs[6:]
    gp = pl.program_id(0)

    @pl.when(gp == 0)
    def _():
        for i in range(4):
            for j in range(4):
                for si in range(2):
                    pack_ref[(at_ref[0] + i) & 3, (at_ref[1] + j) & 3, si] = parts[i][j, si]

    row = lax.broadcasted_iota(jnp.int32, (2 * QB, CB), 0)
    col = lax.broadcasted_iota(jnp.int32, (2 * QB, CB), 1)
    a = row % QB
    pick = (
        (col % 8 == (gp * 2 + row // QB) * 2 + a % 2)
        & (col // 16 % 4 == a // 8)
        & (col // 64 == a % 8 // 2)
    )
    pick = jnp.where(pick, 1.0, 0.0).astype(BF16)
    a = a[:QB]
    ahead = (col[:QB] - (a % 8 // 2 * 8 + a // 8 * 2 + a % 2)).astype(F32)
    wq = jnp.concatenate([wq_ref[0], wq_ref[1]], axis=1)
    xs, qs = [[], []], [[], []]
    for si in range(2):
        rows = jnp.concatenate([packed(pack_ref, si, PQ_AT + p * 16) for p in range(GROUP)], axis=1)
        raw = split2(mm(rows, wq))
        both = mm(pick, rows)
        start = pack_ref[0, 0, si, START_AT:START_AT + 16, :].astype(F32)[0:1, 0:1]
        live = ahead <= start
        for gg in range(2):
            g = gp * 2 + gg
            ks = [packed(pack_ref, si, pl.multiple_of(g * 64 + p * 16, 16)) for p in range(4)]
            mean = wk_ref[gg, 2 * HD:, :]
            proj_k = mm(jnp.concatenate(ks[:2], axis=1), wk_ref[gg, :2 * HD, :])
            proj_k = proj_k + mm(jnp.concatenate(ks[2:], axis=1), jnp.concatenate([mean, mean], axis=0))
            xs[gg].append(both[gg * QB:(gg + 1) * QB])
            mine, lanes = pick[gg * QB:(gg + 1) * QB], slice(gg * HD, (gg + 1) * HD)
            proj_q = mm(mine, raw[0][:, lanes]) + mm(mine, raw[1][:, lanes])
            qs[gg].append(proj_q)
            proj_k = split2(proj_k)
            kh_ref[gg, si * CB:(si + 1) * CB, :] = proj_k[0]
            kl_ref[gg, si * CB:(si + 1) * CB, :] = proj_k[1]
            logits = mm3(split2(proj_q), proj_k, NT) * SCALE
            masked = jnp.where(live, logits, NEG)
            top = masked.max(axis=1, keepdims=True)
            ex = jnp.where(live, jnp.exp(masked - top), 0.0)
            total = ex.sum(axis=1, keepdims=True)
            gate_ref[gg, si * QB:(si + 1) * QB, :] = ex / total
            if si == 0:
                log_ref[gg] = jnp.where(live, masked - top - jnp.log(total), 0.0)
    for gg in range(2):
        hi, lo = split2(jnp.concatenate(xs[gg], axis=0).T)
        xh_ref[gg] = hi
        xl_ref[gg] = lo
        hi, lo = split2(jnp.concatenate(qs[gg], axis=0).T)
        qh_ref[gg] = hi
        ql_ref[gg] = lo


def pair_spec(shape):
    return pl.BlockSpec((2,) + tuple(shape[1:]), lambda g: (g,) + (0,) * (len(shape) - 1))


def whole_spec(shape):
    return pl.BlockSpec(tuple(shape), lambda g: (0,) * len(shape))


def gate_part(at, parts, wq, wk):
    pack = (4, 4, 2, PACK, HD)
    shapes = [(2 * QB, CB), (QB, CB)] + [(GROUP * HD, 2 * QB)] * 2 + [(2 * CB, HD)] * 2 + [(HD, 2 * QB)] * 2
    shapes = [(4,) + s for s in shapes]
    return pl.pallas_call(
        gate_kernel,
        grid=(2,),
        in_specs=[pl.BlockSpec(memory_space=pltpu.SMEM)]
        + [whole_spec(v.shape) for v in parts]
        + [pair_spec(wq.shape), pair_spec(wk.shape)],
        out_specs=[whole_spec(pack)] + [pair_spec(s) for s in shapes],
        out_shape=[jax.ShapeDtypeStruct(pack, BF16)]
        + [jax.ShapeDtypeStruct(s, F32 if i < 2 else BF16) for i, s in enumerate(shapes)],
        compiler_params=pltpu.CompilerParams(vmem_limit_bytes=VMEM),
        cost_estimate=pl.CostEstimate(flops=10 ** 10, bytes_accessed=10 ** 7, transcendentals=10 ** 6),
        name="gate",
    )(at, *parts, wq, wk)


def grads_kernel(y_ref, pack_ref, t_ref, gate_ref, log_ref, xh_ref, xl_ref, kh_ref, kl_ref, qh_ref, ql_ref, g_ref, loss_ref):
    gp = pl.program_id(0)
    wide = GROUP * HD
    for gg in range(2):
        g = gp * 2 + gg
        d_q, d_k = [], []
        for si in range(2):
            yy = y_ref[0] ^ si
            teacher = jnp.concatenate(
                [
                    jnp.concatenate([t_ref[z, x, yy, 0, :, gg * 64:gg * 64 + 64] for z in range(4)], axis=1)
                    for x in range(4)
                ],
                axis=0,
            )
            target = teacher / teacher.sum(axis=1, keepdims=True)
            at = slice(si * QB, (si + 1) * QB)
            if si == 0:
                some = target > 0.0
                term = jnp.where(some, target * jnp.log(jnp.where(some, target, 1.0)), 0.0)
                term = term - target * log_ref[gg]
                loss = term.sum(axis=1, keepdims=True).sum(axis=0, keepdims=True) * (1.0 / QB)
                loss_ref[0, gg:gg + 1, :] = jnp.broadcast_to(loss, (1, 128))
            slope = split2((gate_ref[gg, at, :] - target) * (SCALE / QB))
            ks = slice(si * CB, (si + 1) * CB)
            d_q.append(mm3(slope, (kh_ref[gg, ks, :], kl_ref[gg, ks, :])))
            d_k.append(mm3((qh_ref[gg, :, at], ql_ref[gg, :, at]), slope))
        d_q = split2(jnp.concatenate(d_q, axis=0))
        g_ref[gg, :wide, :] = mm3((xh_ref[gg], xl_ref[gg]), d_q)
        d_k = jnp.concatenate(split2(jnp.concatenate(d_k, axis=1)), axis=0)
        rows = [
            jnp.concatenate([packed(pack_ref, si, pl.multiple_of(g * 64 + p * 16, 16)) for si in range(2)], axis=0)
            for p in range(4)
        ]
        ends = mm(d_k, jnp.concatenate(rows[:2], axis=1))
        mean = mm(d_k, jnp.concatenate(rows[2:], axis=1))
        ends = ends[:HD] + ends[HD:]
        mean = mean[:HD, :HD] + (mean[HD:, :HD] + mean[:HD, HD:])
        g_ref[gg, wide:wide + HD, :] = ends[:, :HD].T
        g_ref[gg, wide + HD:wide + 2 * HD, :] = ends[:, HD:].T
        g_ref[gg, wide + 2 * HD:, :] = mean.T


def gradients(y, pack, teachers, parts):
    out = (4, (GROUP + 3) * HD, HD)
    return pl.pallas_call(
        grads_kernel,
        grid=(2,),
        in_specs=[
            pl.BlockSpec(memory_space=pltpu.SMEM),
            whole_spec(pack.shape),
            pl.BlockSpec((4, 4, 2, 1, 8, 128), lambda g: (0, 0, 0, g, 0, 0)),
        ]
        + [pair_spec(v.shape) for v in parts],
        out_specs=[pair_spec(out), pl.BlockSpec((1, 2, 128), lambda g: (g, 0, 0))],
        out_shape=[jax.ShapeDtypeStruct(out, F32), jax.ShapeDtypeStruct((2, 2, 128), F32)],
        compiler_params=pltpu.CompilerParams(vmem_limit_bytes=VMEM),
        name="gradients",
    )(y, pack, teachers, *parts)


def add_kernel(a_ref, b_ref, q_ref, k_ref):
    wide = q_ref.shape[1]
    q_ref[...] = a_ref[:, :wide] + b_ref[:, :wide]
    k_ref[...] = a_ref[:, wide:] + b_ref[:, wide:]


def add_cores(a, b):
    wide = GROUP * HD
    shapes = [(4, wide, HD), (4, a.shape[1] - wide, HD)]
    return pl.pallas_call(
        add_kernel,
        grid=(2,),
        in_specs=[pair_spec(a.shape)] * 2,
        out_specs=[pair_spec(s) for s in shapes],
        out_shape=[jax.ShapeDtypeStruct(s, F32) for s in shapes],
        compiler_params=pltpu.CompilerParams(vmem_limit_bytes=VMEM),
        name="add_cores",
    )(a, b)


def shift(x, axis, by):
    return lax.ppermute(x, axis, [(i, (i + by) % 4) for i in range(4)])


def swap(x, axis):
    return lax.ppermute(x, axis, [(0, 1), (1, 0)])


def ring(v, axis):
    return [v, shift(v, axis, 1), shift(v, axis, -1), shift(v, axis, 2)]


def upward(parts):
    return [parts[0], parts[2], parts[3], parts[1]]


def per_device(queries, keys, start_block, lengths, gate_query, gate_key):
    del lengths
    z, x, y = lax.axis_index("z"), lax.axis_index("x"), lax.axis_index("y")
    q, k = queries[0], keys[0]
    start = start_block[0]
    half_q, half_k = 2 * GROUP * HD, 2 * HD
    q_parts = ring(q, "z")
    k_before, k_after = shift(k, "x", 1), shift(k, "x", -1)
    k_last, *_ = lax.optimization_barrier((k, k_before, k_after))
    k_far = shift(k_last, "x", 2)
    pack = pool(start_block, q, k)
    pack = ring(jnp.stack([pack, swap(pack, "y")]), "x")
    offs = (0, 3, 1, 2)
    q_pos = [start + (i * 4 + x) * 2 for i in range(4)]
    k_pos = [(z * 4 + ((x + o) & 3)) * 16 for o in offs]
    ints = lambda *v: jnp.stack([jnp.asarray(i, jnp.int32) for i in v])
    q_at = [((z + o) & 3) * 128 for o in offs]
    bm0, ml, qs = block_scores(ints(*q_pos, k_pos[0], *q_at), q_parts, [k])
    pack, bm0 = lax.optimization_barrier((pack, bm0))
    packs = upward(ring(jnp.stack(upward(pack)), "z"))
    bm1, ml = block_scores(ints(*q_pos, *k_pos[1:3]), [qs], [k_before, k_after], [ml])
    bm2, ml = block_scores(ints(*q_pos, k_pos[3]), [qs], [k_far], [ml])
    mls = ring(ml, "z")
    packs, _ = lax.optimization_barrier((packs, ml))
    pack, *parts = gate_part(ints(z, x), packs, gate_query, gate_key)
    parts, mls = lax.optimization_barrier((parts, mls))
    teachers = teacher_blocks(ints(x), [bm0, bm1, bm2], mls, 32)
    teachers = lax.all_to_all(teachers, ("z", "x", "y"), 0, 0, tiled=True).reshape(4, 4, 2, 2, 8, 128)
    grads, loss = gradients(ints(y), pack, teachers, parts)
    grad_q, grad_k = add_cores(grads, swap(grads, "c"))
    return grad_q, grad_k, loss[:, :, 0].reshape(1, 4)


def solution(mesh):
    fine = Mesh(mesh.devices.reshape(4, 4, 2, 2, 2), ("z", "x", "h", "y", "c"))
    ctx, dp = ("z", "x"), ("y", "c")
    placed = (
        P(dp, ctx, "h"),
        P(dp, ctx, "h"),
        P(dp),
        P(dp),
        P("h", None, None),
        P("h", None, None),
    )
    return jax.shard_map(
        per_device,
        mesh=fine,
        in_specs=placed,
        out_specs=(P("h", None, None), P("h", None, None), P(dp, "h")),
        check_vma=False,
    )
```

```python
import functools
import itertools
import math

import jax
import jax.numpy as jnp
from jax import lax
from jax.experimental import pallas as pl
from jax.experimental.pallas import tpu as pltpu
from jax.sharding import Mesh, PartitionSpec as P

BLK = 64
GROUP = 5
HD = 128
QB = 32
CB = 256
NEG = -1e30
FLOOR = -1e20
KT = 512
KB = KT // BLK
SAFE = 100.0
SCALE = HD ** -0.5
SCALE2 = SCALE * math.log2(math.e)
VMEM = 56 * 2 ** 20
F32 = jnp.float32
BF16 = jnp.bfloat16
NT = (((1,), (1,)), ((), ()))
TN = (((0,), (0,)), ((), ()))
NN = (((1,), (0,)), ((), ()))
PQ_AT = 256
START_AT = PQ_AT + 80
PACK = START_AT + 16


def split2(x):
    hi = x.astype(BF16)
    return hi, (x - hi.astype(F32)).astype(BF16)


def mm(a, b, dims=NN):
    return lax.dot_general(a, b, dims, preferred_element_type=F32)


def mm3(a, b, dims=NN):
    return mm(a[0], b[0], dims) + (mm(a[0], b[1], dims) + mm(a[1], b[0], dims))


def block_tops(s):
    return s.reshape(s.shape[0] // BLK, 8, 8, s.shape[1]).max(axis=1).max(axis=1)


def part_sums(s, m):
    return jnp.exp2(s - m).reshape(s.shape[0] // 8, 8, s.shape[1]).sum(axis=0)


def scores_kernel(pos_ref, *refs, n_q, shards):
    refs, nk = list(refs), len(shards)
    take = lambda n: [refs.pop(0) for _ in range(n)]
    q_refs, k_refs = take(n_q), take(nk)
    first = n_q > 1
    ml_in = [] if first else take(1)
    bm_ref, ml_ref = take(2)
    qs = take(1)[0] if first else q_refs[0]
    d_s, bad_s = refs
    rt, piece = qs.shape[2], k_refs[0].shape[0]
    q_pos = [pos_ref[i] for i in range(4)]
    kp = [pos_ref[4 + i] for i in shards]
    if first:
        for i, r in enumerate(q_refs):
            at = pl.multiple_of(pos_ref[8 + i], 128)
            for h in range(GROUP):
                hi, lo = split2(r[:, h * HD:(h + 1) * HD].astype(F32) * SCALE2)
                qs[0, h, pl.ds(at, 128), :] = jnp.concatenate([hi, lo], axis=1)
    tiles = [(p, o) for p in range(nk) for o in range(0, piece, KT)]
    low, high = functools.reduce(jnp.minimum, q_pos), functools.reduce(jnp.maximum, q_pos)
    full = [k + piece // BLK - 1 < low for k in kp]
    none = functools.reduce(jnp.minimum, kp) > high + 1

    def scores(t, h):
        p, o = tiles[t]
        k = k_refs[p][o:o + KT, :]
        return mm(jnp.concatenate([k, k], axis=1), qs[0, h], NT)

    def seen(p):
        lane = lax.broadcasted_iota(jnp.int32, (8, rt), 1)
        d = lane % 128 - lax.broadcasted_iota(jnp.int32, (8, rt), 0)
        for i, v in enumerate(q_pos):
            d = d + jnp.where(lane // 128 == i, (v - kp[p]) * BLK, 0)
        return d

    def masked(t, h):
        p, o = tiles[t]
        keep = jnp.concatenate([d_s[p] >= o + i for i in range(0, KT, 8)], axis=0)
        return jnp.where(keep, scores(t, h), NEG)

    def store(h, found):
        if ml_in:
            m = ml_in[0][0, h, 0:1, :]
            found = found + [(m, m, ml_in[0][0, h, 1:2, :])]
        big = functools.reduce(jnp.maximum, [f[1] for f in found])
        ml_ref[0, h, 0:1, :] = big
        ml_ref[0, h, 1:2, :] = sum(f[2] * jnp.exp2(f[0] - big) for f in found)

    def heads(masks):
        for p in range(nk):
            if masks[p]:
                d_s[p] = seen(p)

        def head(h, worst):
            found = []
            for t, (p, o) in enumerate(tiles):
                s = masked(t, h) if masks[p] else scores(t, h)
                if t == 0 or (o == 0 and (masks[p] or masks[p - 1])):
                    m = s[:BLK].reshape(8, 8, rt).max(axis=0).max(axis=0, keepdims=True)
                    m = jnp.maximum(m, FLOOR) if masks[p] else m
                    found.append([m, m, None])
                top, part = block_tops(s), part_sums(s, m)
                bm_ref[0, h, t * KB:(t + 1) * KB, :] = top
                f = found[-1]
                f[1] = jnp.maximum(f[1], top.max(axis=0, keepdims=True))
                f[2] = part if f[2] is None else f[2] + part
            store(h, [(f[0], f[1], f[2].sum(axis=0, keepdims=True)) for f in found])
            return functools.reduce(jnp.maximum, [f[1] - f[0] for f in found], worst)

        worst = jnp.zeros((1, rt), F32)
        if nk == 1 or not any(masks):
            for h in range(GROUP):
                worst = head(h, worst)
        else:
            worst = lax.fori_loop(0, GROUP, head, worst)
        bad_s[0] = jnp.max(worst)

    for masks in itertools.product((False, True), repeat=nk):
        match = functools.reduce(jnp.logical_and, [f != m for f, m in zip(full, masks)])
        pl.when(match & jnp.logical_not(none))(functools.partial(heads, masks))

    @pl.when(none)
    def _():
        bm_ref[...] = jnp.full(bm_ref.shape, NEG, F32)
        for h in range(GROUP):
            store(h, [(jnp.full((1, rt), FLOOR, F32), jnp.full((1, rt), FLOOR, F32), jnp.zeros((1, rt), F32))])
        bad_s[0] = 0.0

    @pl.when(bad_s[0] > SAFE)
    def _():
        for p in range(nk):
            d_s[p] = seen(p)

        def head(h, _):
            m, l = jnp.full((1, rt), FLOOR, F32), jnp.zeros((8, rt), F32)
            for t in range(len(tiles)):
                s = masked(t, h)
                top = block_tops(s)
                bm_ref[0, h, t * KB:(t + 1) * KB, :] = top
                new = jnp.maximum(m, top.max(axis=0, keepdims=True))
                l = l * jnp.exp2(m - new) + part_sums(s, new)
                m = new
            store(h, [(m, m, l.sum(axis=0, keepdims=True))])
            return 0

        lax.fori_loop(0, GROUP, head, 0)


def block_scores(pos, q_parts, k_parts, shards, ml_in=()):
    first = len(q_parts) > 1
    rt, kn = 512, sum(k.shape[0] for k in k_parts)
    groups = k_parts[0].shape[1] // HD
    per_group = lambda s: pl.BlockSpec((1,) + tuple(s[1:]), lambda g, p: (g, 0, 0, 0))
    lanes = lambda v: pl.BlockSpec((v.shape[0], v.shape[1] // groups), lambda g, p: (0, g))
    shapes = [(groups, GROUP, kn // BLK, rt), (groups, GROUP, 2, rt)] + [(groups, GROUP, rt, 2 * HD)] * first
    return pl.pallas_call(
        functools.partial(scores_kernel, n_q=len(q_parts), shards=shards),
        grid_spec=pltpu.PrefetchScalarGridSpec(
            num_scalar_prefetch=1,
            grid=(groups,),
            in_specs=[lanes(q) if first else per_group(q.shape) for q in q_parts]
            + [lanes(k) for k in k_parts]
            + [per_group(m.shape) for m in ml_in],
            out_specs=[per_group(s) for s in shapes],
            scratch_shapes=[pltpu.VMEM((len(k_parts), 8, rt), jnp.int32), pltpu.SMEM((1,), F32)],
        ),
        out_shape=[jax.ShapeDtypeStruct(s, t) for s, t in zip(shapes, (F32, F32, BF16))],
        compiler_params=pltpu.CompilerParams(vmem_limit_bytes=VMEM),
        name="block_scores",
    )(pos, *q_parts, *k_parts, *ml_in)


def pool_kernel(start_ref, q_ref, k_ref, out_ref):
    groups = k_ref.shape[1] // HD
    for g in range(groups):
        x = k_ref[:, g * HD:(g + 1) * HD].astype(F32).reshape(16, BLK, HD)
        hi, lo = split2(x.sum(axis=1) * (1.0 / BLK))
        parts = [x.max(axis=1).astype(BF16), x.min(axis=1).astype(BF16), hi, lo]
        for p, part in enumerate(parts):
            out_ref[g * 64 + p * 16:g * 64 + p * 16 + 16, :] = part
    for p in range(GROUP):
        rows = []
        for g in range(groups):
            at = (g * GROUP + p) * HD
            x = q_ref[:, at:at + HD].astype(F32).reshape(2, BLK, HD)
            rows.append(x.sum(axis=1) * (1.0 / BLK))
        hi, lo = split2(jnp.concatenate(rows, axis=0))
        at = PQ_AT + p * 16
        out_ref[at:at + 16, :] = jnp.concatenate([hi.astype(F32), lo.astype(F32)], axis=0).astype(BF16)
    out_ref[START_AT:, :] = jnp.full((16, HD), start_ref[0].astype(F32), F32).astype(BF16)


def pool(start_block, q, k):
    return pl.pallas_call(
        pool_kernel,
        in_specs=[
            pl.BlockSpec(memory_space=pltpu.SMEM),
            pl.BlockSpec(memory_space=pltpu.VMEM),
            pl.BlockSpec(memory_space=pltpu.VMEM),
        ],
        out_specs=pl.BlockSpec(memory_space=pltpu.VMEM),
        out_shape=jax.ShapeDtypeStruct((PACK, HD), BF16),
        compiler_params=pltpu.CompilerParams(vmem_limit_bytes=VMEM),
        name="pool",
    )(start_block, q, k)


def teacher_kernel(x_ref, *refs):
    near, sides, far = refs[:3]
    ml_refs, (out_ref, sc) = refs[3:-2], refs[-2:]
    rt = near.shape[3]
    to = [pl.multiple_of(((x_ref[0] + o) & 3) * 16, 16) for o in (0, 3, 1, 2)]
    for g in range(4):
        for h in range(GROUP):
            ms = [m[g, h, 0:1, :] for m in ml_refs]
            m = functools.reduce(jnp.maximum, ms)
            l = sum(ref[g, h, 1:2, :] * jnp.exp2(mi - m) for ref, mi in zip(ml_refs, ms))
            lse = m + jnp.log(l) * math.log2(math.e)
            parts = [near[g, h], sides[g, h, :16], sides[g, h, 16:], far[g, h]]
            for at, v in zip(to, parts):
                sc[g // 2 * GROUP + h, pl.ds(at + g % 2 * 64, 16), :] = v - lse
    for gp in range(2):
        totals = [None] * (rt // 128)
        for h in range(GROUP):
            for i in range(rt // 128):
                t = sc[gp * GROUP + h, :, i * 128:(i + 1) * 128].T
                top = jnp.exp2(t.reshape(2, BLK, 128).max(axis=1))
                totals[i] = top if h == 0 else totals[i] + top
        tile = jnp.concatenate(totals, axis=0) * (1.0 / GROUP)
        out_ref[:, gp] = jnp.broadcast_to(tile[None], (out_ref.shape[0],) + tile.shape)


def teacher_blocks(x, bms, mls, copies):
    return pl.pallas_call(
        teacher_kernel,
        in_specs=[pl.BlockSpec(memory_space=pltpu.SMEM)]
        + [pl.BlockSpec(memory_space=pltpu.VMEM)] * (len(bms) + len(mls)),
        out_specs=pl.BlockSpec(memory_space=pltpu.VMEM),
        out_shape=jax.ShapeDtypeStruct((copies, 2, 8, 128), F32),
        scratch_shapes=[pltpu.VMEM((2 * GROUP, 128, bms[0].shape[3]), F32)],
        compiler_params=pltpu.CompilerParams(vmem_limit_bytes=VMEM),
        name="teacher",
    )(x, *bms, *mls)


def packed(pack_ref, si, at):
    return pack_ref[:, :, si, pl.ds(at, 16), :].reshape(CB, HD)


def gate_kernel(at_ref, *refs):
    parts, (wq_ref, wk_ref) = refs[:4], refs[4:6]
    pack_ref, gate_ref, log_ref, xh_ref, xl_ref, kh_ref, kl_ref, qh_ref, ql_ref = refs[6:]
    gp = pl.program_id(0)

    @pl.when(gp == 0)
    def _():
        for i in range(4):
            for j in range(4):
                for si in range(2):
                    pack_ref[(at_ref[0] + i) & 3, (at_ref[1] + j) & 3, si] = parts[i][j, si]

    row = lax.broadcasted_iota(jnp.int32, (2 * QB, CB), 0)
    col = lax.broadcasted_iota(jnp.int32, (2 * QB, CB), 1)
    a = row % QB
    pick = (
        (col % 8 == (gp * 2 + row // QB) * 2 + a % 2)
        & (col // 16 % 4 == a // 8)
        & (col // 64 == a % 8 // 2)
    )
    pick = jnp.where(pick, 1.0, 0.0).astype(BF16)
    a = a[:QB]
    ahead = (col[:QB] - (a % 8 // 2 * 8 + a // 8 * 2 + a % 2)).astype(F32)
    wq = jnp.concatenate([wq_ref[0], wq_ref[1]], axis=1)
    xs, qs = [[], []], [[], []]
    for si in range(2):
        rows = jnp.concatenate([packed(pack_ref, si, PQ_AT + p * 16) for p in range(GROUP)], axis=1)
        raw = split2(mm(rows, wq))
        both = mm(pick, rows)
        start = pack_ref[0, 0, si, START_AT:START_AT + 16, :].astype(F32)[0:1, 0:1]
        live = ahead <= start
        for gg in range(2):
            g = gp * 2 + gg
            ks = [packed(pack_ref, si, pl.multiple_of(g * 64 + p * 16, 16)) for p in range(4)]
            mean = wk_ref[gg, 2 * HD:, :]
            proj_k = mm(jnp.concatenate(ks[:2], axis=1), wk_ref[gg, :2 * HD, :])
            proj_k = proj_k + mm(jnp.concatenate(ks[2:], axis=1), jnp.concatenate([mean, mean], axis=0))
            xs[gg].append(both[gg * QB:(gg + 1) * QB])
            mine, lanes = pick[gg * QB:(gg + 1) * QB], slice(gg * HD, (gg + 1) * HD)
            proj_q = mm(mine, raw[0][:, lanes]) + mm(mine, raw[1][:, lanes])
            qs[gg].append(proj_q)
            proj_k = split2(proj_k)
            kh_ref[gg, si * CB:(si + 1) * CB, :] = proj_k[0]
            kl_ref[gg, si * CB:(si + 1) * CB, :] = proj_k[1]
            logits = mm3(split2(proj_q), proj_k, NT) * SCALE
            masked = jnp.where(live, logits, NEG)
            top = masked.max(axis=1, keepdims=True)
            ex = jnp.where(live, jnp.exp(masked - top), 0.0)
            total = ex.sum(axis=1, keepdims=True)
            gate_ref[gg, si * QB:(si + 1) * QB, :] = ex / total
            if si == 0:
                log_ref[gg] = jnp.where(live, masked - top - jnp.log(total), 0.0)
    for gg in range(2):
        hi, lo = split2(jnp.concatenate(xs[gg], axis=0).T)
        xh_ref[gg] = hi
        xl_ref[gg] = lo
        hi, lo = split2(jnp.concatenate(qs[gg], axis=0).T)
        qh_ref[gg] = hi
        ql_ref[gg] = lo


def pair_spec(shape):
    return pl.BlockSpec((2,) + tuple(shape[1:]), lambda g: (g,) + (0,) * (len(shape) - 1))


def whole_spec(shape):
    return pl.BlockSpec(tuple(shape), lambda g: (0,) * len(shape))


def gate_part(at, parts, wq, wk):
    pack = (4, 4, 2, PACK, HD)
    shapes = [(2 * QB, CB), (QB, CB)] + [(GROUP * HD, 2 * QB)] * 2 + [(2 * CB, HD)] * 2 + [(HD, 2 * QB)] * 2
    shapes = [(4,) + s for s in shapes]
    return pl.pallas_call(
        gate_kernel,
        grid=(2,),
        in_specs=[pl.BlockSpec(memory_space=pltpu.SMEM)]
        + [whole_spec(v.shape) for v in parts]
        + [pair_spec(wq.shape), pair_spec(wk.shape)],
        out_specs=[whole_spec(pack)] + [pair_spec(s) for s in shapes],
        out_shape=[jax.ShapeDtypeStruct(pack, BF16)]
        + [jax.ShapeDtypeStruct(s, F32 if i < 2 else BF16) for i, s in enumerate(shapes)],
        compiler_params=pltpu.CompilerParams(vmem_limit_bytes=VMEM),
        cost_estimate=pl.CostEstimate(flops=10 ** 10, bytes_accessed=10 ** 7, transcendentals=10 ** 6),
        name="gate",
    )(at, *parts, wq, wk)


def grads_kernel(y_ref, pack_ref, t_ref, gate_ref, log_ref, xh_ref, xl_ref, kh_ref, kl_ref, qh_ref, ql_ref, g_ref, loss_ref):
    gp = pl.program_id(0)
    wide = GROUP * HD
    for gg in range(2):
        g = gp * 2 + gg
        d_q, d_k = [], []
        for si in range(2):
            yy = y_ref[0] ^ si
            teacher = jnp.concatenate(
                [
                    jnp.concatenate([t_ref[z, x, yy, 0, :, gg * 64:gg * 64 + 64] for z in range(4)], axis=1)
                    for x in range(4)
                ],
                axis=0,
            )
            target = teacher / teacher.sum(axis=1, keepdims=True)
            at = slice(si * QB, (si + 1) * QB)
            if si == 0:
                some = target > 0.0
                term = jnp.where(some, target * jnp.log(jnp.where(some, target, 1.0)), 0.0)
                term = term - target * log_ref[gg]
                loss = term.sum(axis=1, keepdims=True).sum(axis=0, keepdims=True) * (1.0 / QB)
                loss_ref[0, gg:gg + 1, :] = jnp.broadcast_to(loss, (1, 128))
            slope = split2((gate_ref[gg, at, :] - target) * (SCALE / QB))
            ks = slice(si * CB, (si + 1) * CB)
            d_q.append(mm3(slope, (kh_ref[gg, ks, :], kl_ref[gg, ks, :])))
            d_k.append(mm3((qh_ref[gg, :, at], ql_ref[gg, :, at]), slope))
        d_q = split2(jnp.concatenate(d_q, axis=0))
        g_ref[gg, :wide, :] = mm3((xh_ref[gg], xl_ref[gg]), d_q)
        d_k = jnp.concatenate(split2(jnp.concatenate(d_k, axis=1)), axis=0)
        rows = [
            jnp.concatenate([packed(pack_ref, si, pl.multiple_of(g * 64 + p * 16, 16)) for si in range(2)], axis=0)
            for p in range(4)
        ]
        ends = mm(d_k, jnp.concatenate(rows[:2], axis=1))
        mean = mm(d_k, jnp.concatenate(rows[2:], axis=1))
        ends = ends[:HD] + ends[HD:]
        mean = mean[:HD, :HD] + (mean[HD:, :HD] + mean[:HD, HD:])
        g_ref[gg, wide:wide + HD, :] = ends[:, :HD].T
        g_ref[gg, wide + HD:wide + 2 * HD, :] = ends[:, HD:].T
        g_ref[gg, wide + 2 * HD:, :] = mean.T


def gradients(y, pack, teachers, parts):
    out = (4, (GROUP + 3) * HD, HD)
    return pl.pallas_call(
        grads_kernel,
        grid=(2,),
        in_specs=[
            pl.BlockSpec(memory_space=pltpu.SMEM),
            whole_spec(pack.shape),
            pl.BlockSpec((4, 4, 2, 1, 8, 128), lambda g: (0, 0, 0, g, 0, 0)),
        ]
        + [pair_spec(v.shape) for v in parts],
        out_specs=[pair_spec(out), pl.BlockSpec((1, 2, 128), lambda g: (g, 0, 0))],
        out_shape=[jax.ShapeDtypeStruct(out, F32), jax.ShapeDtypeStruct((2, 2, 128), F32)],
        compiler_params=pltpu.CompilerParams(vmem_limit_bytes=VMEM),
        name="gradients",
    )(y, pack, teachers, *parts)


def add_kernel(a_ref, b_ref, q_ref, k_ref):
    wide = q_ref.shape[1]
    q_ref[...] = a_ref[:, :wide] + b_ref[:, :wide]
    k_ref[...] = a_ref[:, wide:] + b_ref[:, wide:]


def add_cores(a, b):
    wide = GROUP * HD
    shapes = [(4, wide, HD), (4, a.shape[1] - wide, HD)]
    return pl.pallas_call(
        add_kernel,
        grid=(2,),
        in_specs=[pair_spec(a.shape)] * 2,
        out_specs=[pair_spec(s) for s in shapes],
        out_shape=[jax.ShapeDtypeStruct(s, F32) for s in shapes],
        compiler_params=pltpu.CompilerParams(vmem_limit_bytes=VMEM),
        name="add_cores",
    )(a, b)


def shift(x, axis, by):
    return lax.ppermute(x, axis, [(i, (i + by) % 4) for i in range(4)])


def swap(x, axis):
    return lax.ppermute(x, axis, [(0, 1), (1, 0)])


def ring(v, axis):
    return [v, shift(v, axis, 1), shift(v, axis, -1), shift(v, axis, 2)]


def upward(parts):
    return [parts[0], parts[2], parts[3], parts[1]]


def per_device(queries, keys, start_block, lengths, gate_query, gate_key):
    del lengths
    z, x, y = lax.axis_index("z"), lax.axis_index("x"), lax.axis_index("y")
    q, k = queries[0], keys[0]
    start = start_block[0]
    half_q, half_k = 2 * GROUP * HD, 2 * HD
    q_parts = ring(q, "z")
    k_before, k_after = shift(k, "x", 1), shift(k, "x", -1)
    pack = pool(start_block, q, k)
    pack = ring(jnp.stack([pack, swap(pack, "y")]), "x")
    offs = (0, 3, 1, 2)
    q_pos = [start + (i * 4 + x) * 2 for i in range(4)]
    k_pos = [(z * 4 + ((x + o) & 3)) * 16 for o in offs]
    ints = lambda *v: jnp.stack([jnp.asarray(i, jnp.int32) for i in v])
    q_at = [((z + o) & 3) * 128 for o in offs]
    pos = ints(*q_pos, *k_pos, *q_at)
    bm0, ml, qs = block_scores(pos, q_parts, [k], (0,))
    pack, bm0, k_last = lax.optimization_barrier((pack, bm0, k))
    k_far = shift(k_last, "x", 2)
    packs = upward(ring(jnp.stack(upward(pack)), "z"))
    bm1, ml = block_scores(pos, [qs], [k_before, k_after], (1, 2), [ml])
    bm2, ml = block_scores(pos, [qs], [k_far], (3,), [ml])
    mls = ring(ml, "z")
    packs, _ = lax.optimization_barrier((packs, ml))
    pack, *parts = gate_part(ints(z, x), packs, gate_query, gate_key)
    parts, mls = lax.optimization_barrier((parts, mls))
    teachers = teacher_blocks(ints(x), [bm0, bm1, bm2], mls, 32)
    teachers = lax.all_to_all(teachers, ("z", "x", "y"), 0, 0, tiled=True).reshape(4, 4, 2, 2, 8, 128)
    grads, loss = gradients(ints(y), pack, teachers, parts)
    grad_q, grad_k = add_cores(grads, swap(grads, "c"))
    return grad_q, grad_k, loss[:, :, 0].reshape(1, 4)


def solution(mesh):
    fine = Mesh(mesh.devices.reshape(4, 4, 2, 2, 2), ("z", "x", "h", "y", "c"))
    ctx, dp = ("z", "x"), ("y", "c")
    placed = (
        P(dp, ctx, "h"),
        P(dp, ctx, "h"),
        P(dp),
        P(dp),
        P("h", None, None),
        P("h", None, None),
    )
    return jax.shard_map(
        per_device,
        mesh=fine,
        in_specs=placed,
        out_specs=(P("h", None, None), P("h", None, None), P(dp, "h")),
        check_vma=False,
    )
```

```python
import functools
import itertools
import math

import jax
import jax.numpy as jnp
from jax import lax
from jax.experimental import pallas as pl
from jax.experimental.pallas import tpu as pltpu
from jax.sharding import Mesh, PartitionSpec as P

BLK = 64
GROUP = 5
HD = 128
QB = 32
CB = 256
NEG = -1e30
FLOOR = -1e20
KT = 512
KB = KT // BLK
SAFE = 100.0
SCALE = HD ** -0.5
SCALE2 = SCALE * math.log2(math.e)
VMEM = 56 * 2 ** 20
F32 = jnp.float32
BF16 = jnp.bfloat16
NT = (((1,), (1,)), ((), ()))
TN = (((0,), (0,)), ((), ()))
NN = (((1,), (0,)), ((), ()))
PQ_AT = 256
START_AT = PQ_AT + 80
PACK = START_AT + 16


def split2(x):
    hi = x.astype(BF16)
    return hi, (x - hi.astype(F32)).astype(BF16)


def mm(a, b, dims=NN):
    return lax.dot_general(a, b, dims, preferred_element_type=F32)


def mm3(a, b, dims=NN):
    return mm(a[0], b[0], dims) + (mm(a[0], b[1], dims) + mm(a[1], b[0], dims))


def block_tops(s):
    return s.reshape(s.shape[0] // BLK, 8, 8, s.shape[1]).max(axis=1).max(axis=1)


def part_sums(s, m):
    return jnp.exp2(s - m).reshape(s.shape[0] // 8, 8, s.shape[1]).sum(axis=0)


def scores_kernel(pos_ref, *refs, n_q, shards):
    refs, nk = list(refs), len(shards)
    take = lambda n: [refs.pop(0) for _ in range(n)]
    q_refs, k_refs = take(n_q), take(nk)
    first = n_q > 1
    ml_in = [] if first else take(1)
    bm_ref, ml_ref = take(2)
    qs = take(1)[0] if first else q_refs[0]
    d_s, bad_s = refs
    rt, piece = qs.shape[2], k_refs[0].shape[0]
    q_pos = [pos_ref[i] for i in range(4)]
    kp = [pos_ref[4 + i] for i in shards]
    if first:
        for i, r in enumerate(q_refs):
            at = pl.multiple_of(pos_ref[8 + i], 128)
            for h in range(GROUP):
                hi, lo = split2(r[:, h * HD:(h + 1) * HD].astype(F32) * SCALE2)
                qs[0, h, pl.ds(at, 128), :] = jnp.concatenate([hi, lo], axis=1)
    tiles = [(p, o) for p in range(nk) for o in range(0, piece, KT)]
    low, high = functools.reduce(jnp.minimum, q_pos), functools.reduce(jnp.maximum, q_pos)
    full = [k + piece // BLK - 1 < low for k in kp]
    none = functools.reduce(jnp.minimum, kp) > high + 1

    def scores(t, h):
        p, o = tiles[t]
        k = k_refs[p][o:o + KT, :]
        return mm(jnp.concatenate([k, k], axis=1), qs[0, h], NT)

    def seen(p):
        lane = lax.broadcasted_iota(jnp.int32, (8, rt), 1)
        d = lane % 128 - lax.broadcasted_iota(jnp.int32, (8, rt), 0)
        for i, v in enumerate(q_pos):
            d = d + jnp.where(lane // 128 == i, (v - kp[p]) * BLK, 0)
        return d

    def masked(t, h):
        p, o = tiles[t]
        keep = jnp.concatenate([d_s[p] >= o + i for i in range(0, KT, 8)], axis=0)
        return jnp.where(keep, scores(t, h), NEG)

    def store(h, found):
        if ml_in:
            m = ml_in[0][0, h, 0:1, :]
            found = found + [(m, m, ml_in[0][0, h, 1:2, :])]
        big = functools.reduce(jnp.maximum, [f[1] for f in found])
        ml_ref[0, h, 0:1, :] = big
        ml_ref[0, h, 1:2, :] = sum(f[2] * jnp.exp2(f[0] - big) for f in found)

    def heads(masks):
        for p in range(nk):
            if masks[p]:
                d_s[p] = seen(p)

        def head(h, worst):
            found = []
            for t, (p, o) in enumerate(tiles):
                s = masked(t, h) if masks[p] else scores(t, h)
                if t == 0 or (o == 0 and (masks[p] or masks[p - 1])):
                    m = s[:BLK].reshape(8, 8, rt).max(axis=0).max(axis=0, keepdims=True)
                    m = jnp.maximum(m, FLOOR) if masks[p] else m
                    found.append([m, m, None])
                top, part = block_tops(s), part_sums(s, m)
                bm_ref[0, h, t * KB:(t + 1) * KB, :] = top
                f = found[-1]
                f[1] = jnp.maximum(f[1], top.max(axis=0, keepdims=True))
                f[2] = part if f[2] is None else f[2] + part
            store(h, [(f[0], f[1], f[2].sum(axis=0, keepdims=True)) for f in found])
            return functools.reduce(jnp.maximum, [f[1] - f[0] for f in found], worst)

        worst = jnp.zeros((1, rt), F32)
        if nk == 1 or not any(masks):
            for h in range(GROUP):
                worst = head(h, worst)
        else:
            worst = lax.fori_loop(0, GROUP, head, worst)
        bad_s[0] = jnp.max(worst)

    for masks in itertools.product((False, True), repeat=nk):
        match = functools.reduce(jnp.logical_and, [f != m for f, m in zip(full, masks)])
        pl.when(match & jnp.logical_not(none))(functools.partial(heads, masks))

    @pl.when(none)
    def _():
        bm_ref[...] = jnp.full(bm_ref.shape, NEG, F32)
        for h in range(GROUP):
            store(h, [(jnp.full((1, rt), FLOOR, F32), jnp.full((1, rt), FLOOR, F32), jnp.zeros((1, rt), F32))])
        bad_s[0] = 0.0

    @pl.when(bad_s[0] > SAFE)
    def _():
        for p in range(nk):
            d_s[p] = seen(p)

        def head(h, _):
            m, l = jnp.full((1, rt), FLOOR, F32), jnp.zeros((8, rt), F32)
            for t in range(len(tiles)):
                s = masked(t, h)
                top = block_tops(s)
                bm_ref[0, h, t * KB:(t + 1) * KB, :] = top
                new = jnp.maximum(m, top.max(axis=0, keepdims=True))
                l = l * jnp.exp2(m - new) + part_sums(s, new)
                m = new
            store(h, [(m, m, l.sum(axis=0, keepdims=True))])
            return 0

        lax.fori_loop(0, GROUP, head, 0)


def block_scores(pos, q_parts, k_parts, shards, ml_in=()):
    first = len(q_parts) > 1
    rt, kn = 512, sum(k.shape[0] for k in k_parts)
    groups = k_parts[0].shape[1] // HD
    per_group = lambda s: pl.BlockSpec((1,) + tuple(s[1:]), lambda g, p: (g, 0, 0, 0))
    lanes = lambda v: pl.BlockSpec((v.shape[0], v.shape[1] // groups), lambda g, p: (0, g))
    shapes = [(groups, GROUP, kn // BLK, rt), (groups, GROUP, 2, rt)] + [(groups, GROUP, rt, 2 * HD)] * first
    return pl.pallas_call(
        functools.partial(scores_kernel, n_q=len(q_parts), shards=shards),
        grid_spec=pltpu.PrefetchScalarGridSpec(
            num_scalar_prefetch=1,
            grid=(groups,),
            in_specs=[lanes(q) if first else per_group(q.shape) for q in q_parts]
            + [lanes(k) for k in k_parts]
            + [per_group(m.shape) for m in ml_in],
            out_specs=[per_group(s) for s in shapes],
            scratch_shapes=[pltpu.VMEM((len(k_parts), 8, rt), jnp.int32), pltpu.SMEM((1,), F32)],
        ),
        out_shape=[jax.ShapeDtypeStruct(s, t) for s, t in zip(shapes, (F32, F32, BF16))],
        compiler_params=pltpu.CompilerParams(vmem_limit_bytes=VMEM),
        name="block_scores",
    )(pos, *q_parts, *k_parts, *ml_in)


def pool_kernel(start_ref, q_ref, k_ref, out_ref):
    groups = k_ref.shape[1] // HD
    for g in range(groups):
        x = k_ref[:, g * HD:(g + 1) * HD].astype(F32).reshape(16, BLK, HD)
        hi, lo = split2(x.sum(axis=1) * (1.0 / BLK))
        parts = [x.max(axis=1).astype(BF16), x.min(axis=1).astype(BF16), hi, lo]
        for p, part in enumerate(parts):
            out_ref[g * 64 + p * 16:g * 64 + p * 16 + 16, :] = part
    for p in range(GROUP):
        rows = []
        for g in range(groups):
            at = (g * GROUP + p) * HD
            x = q_ref[:, at:at + HD].astype(F32).reshape(2, BLK, HD)
            rows.append(x.sum(axis=1) * (1.0 / BLK))
        hi, lo = split2(jnp.concatenate(rows, axis=0))
        at = PQ_AT + p * 16
        out_ref[at:at + 16, :] = jnp.concatenate([hi.astype(F32), lo.astype(F32)], axis=0).astype(BF16)
    out_ref[START_AT:, :] = jnp.full((16, HD), start_ref[0].astype(F32), F32).astype(BF16)


def pool(start_block, q, k):
    return pl.pallas_call(
        pool_kernel,
        in_specs=[
            pl.BlockSpec(memory_space=pltpu.SMEM),
            pl.BlockSpec(memory_space=pltpu.VMEM),
            pl.BlockSpec(memory_space=pltpu.VMEM),
        ],
        out_specs=pl.BlockSpec(memory_space=pltpu.VMEM),
        out_shape=jax.ShapeDtypeStruct((PACK, HD), BF16),
        compiler_params=pltpu.CompilerParams(vmem_limit_bytes=VMEM),
        name="pool",
    )(start_block, q, k)


def teacher_kernel(x_ref, *refs):
    near, sides, far = refs[:3]
    ml_refs, (out_ref, sc) = refs[3:-2], refs[-2:]
    rt = near.shape[3]
    to = [pl.multiple_of(((x_ref[0] + o) & 3) * 16, 16) for o in (0, 3, 1, 2)]
    for g in range(4):
        for h in range(GROUP):
            ms = [m[g, h, 0:1, :] for m in ml_refs]
            m = functools.reduce(jnp.maximum, ms)
            l = sum(ref[g, h, 1:2, :] * jnp.exp2(mi - m) for ref, mi in zip(ml_refs, ms))
            lse = m + jnp.log(l) * math.log2(math.e)
            parts = [near[g, h], sides[g, h, :16], sides[g, h, 16:], far[g, h]]
            for at, v in zip(to, parts):
                sc[g // 2 * GROUP + h, pl.ds(at + g % 2 * 64, 16), :] = v - lse
    for gp in range(2):
        totals = [None] * (rt // 128)
        for h in range(GROUP):
            for i in range(rt // 128):
                t = sc[gp * GROUP + h, :, i * 128:(i + 1) * 128].T
                top = jnp.exp2(t.reshape(2, BLK, 128).max(axis=1))
                totals[i] = top if h == 0 else totals[i] + top
        tile = jnp.concatenate(totals, axis=0) * (1.0 / GROUP)
        out_ref[:, gp] = jnp.broadcast_to(tile[None], (out_ref.shape[0],) + tile.shape)


def teacher_blocks(x, bms, mls, copies):
    return pl.pallas_call(
        teacher_kernel,
        in_specs=[pl.BlockSpec(memory_space=pltpu.SMEM)]
        + [pl.BlockSpec(memory_space=pltpu.VMEM)] * (len(bms) + len(mls)),
        out_specs=pl.BlockSpec(memory_space=pltpu.VMEM),
        out_shape=jax.ShapeDtypeStruct((copies, 2, 8, 128), F32),
        scratch_shapes=[pltpu.VMEM((2 * GROUP, 128, bms[0].shape[3]), F32)],
        compiler_params=pltpu.CompilerParams(vmem_limit_bytes=VMEM),
        name="teacher",
    )(x, *bms, *mls)


def packed(pack_ref, si, at):
    return pack_ref[:, :, si, pl.ds(at, 16), :].reshape(CB, HD)


def gate_kernel(at_ref, *refs):
    parts, (wq_ref, wk_ref) = refs[:4], refs[4:6]
    pack_ref, gate_ref, log_ref, xh_ref, xl_ref, kh_ref, kl_ref, qh_ref, ql_ref = refs[6:]
    gp = pl.program_id(0)

    @pl.when(gp == 0)
    def _():
        for i in range(4):
            for j in range(4):
                for si in range(2):
                    pack_ref[(at_ref[0] + i) & 3, (at_ref[1] + j) & 3, si] = parts[i][j, si]

    row = lax.broadcasted_iota(jnp.int32, (2 * QB, CB), 0)
    col = lax.broadcasted_iota(jnp.int32, (2 * QB, CB), 1)
    a = row % QB
    pick = (
        (col % 8 == (gp * 2 + row // QB) * 2 + a % 2)
        & (col // 16 % 4 == a // 8)
        & (col // 64 == a % 8 // 2)
    )
    pick = jnp.where(pick, 1.0, 0.0).astype(BF16)
    a = a[:QB]
    ahead = (col[:QB] - (a % 8 // 2 * 8 + a // 8 * 2 + a % 2)).astype(F32)
    wq = jnp.concatenate([wq_ref[0], wq_ref[1]], axis=1)
    xs, qs = [[], []], [[], []]
    for si in range(2):
        rows = jnp.concatenate([packed(pack_ref, si, PQ_AT + p * 16) for p in range(GROUP)], axis=1)
        raw = split2(mm(rows, wq))
        both = mm(pick, rows)
        start = pack_ref[0, 0, si, START_AT:START_AT + 16, :].astype(F32)[0:1, 0:1]
        live = ahead <= start
        for gg in range(2):
            g = gp * 2 + gg
            ks = [packed(pack_ref, si, pl.multiple_of(g * 64 + p * 16, 16)) for p in range(4)]
            mean = wk_ref[gg, 2 * HD:, :]
            proj_k = mm(jnp.concatenate(ks[:2], axis=1), wk_ref[gg, :2 * HD, :])
            proj_k = proj_k + mm(jnp.concatenate(ks[2:], axis=1), jnp.concatenate([mean, mean], axis=0))
            xs[gg].append(both[gg * QB:(gg + 1) * QB])
            mine, lanes = pick[gg * QB:(gg + 1) * QB], slice(gg * HD, (gg + 1) * HD)
            proj_q = mm(mine, raw[0][:, lanes]) + mm(mine, raw[1][:, lanes])
            qs[gg].append(proj_q)
            proj_k = split2(proj_k)
            kh_ref[gg, si * CB:(si + 1) * CB, :] = proj_k[0]
            kl_ref[gg, si * CB:(si + 1) * CB, :] = proj_k[1]
            logits = mm3(split2(proj_q), proj_k, NT) * SCALE
            masked = jnp.where(live, logits, NEG)
            top = masked.max(axis=1, keepdims=True)
            ex = jnp.where(live, jnp.exp(masked - top), 0.0)
            total = ex.sum(axis=1, keepdims=True)
            gate_ref[gg, si * QB:(si + 1) * QB, :] = ex / total
            if si == 0:
                log_ref[gg] = jnp.where(live, masked - top - jnp.log(total), 0.0)
    for gg in range(2):
        hi, lo = split2(jnp.concatenate(xs[gg], axis=0).T)
        xh_ref[gg] = hi
        xl_ref[gg] = lo
        hi, lo = split2(jnp.concatenate(qs[gg], axis=0).T)
        qh_ref[gg] = hi
        ql_ref[gg] = lo


def pair_spec(shape):
    return pl.BlockSpec((2,) + tuple(shape[1:]), lambda g: (g,) + (0,) * (len(shape) - 1))


def whole_spec(shape):
    return pl.BlockSpec(tuple(shape), lambda g: (0,) * len(shape))


def gate_part(at, parts, wq, wk):
    pack = (4, 4, 2, PACK, HD)
    shapes = [(2 * QB, CB), (QB, CB)] + [(GROUP * HD, 2 * QB)] * 2 + [(2 * CB, HD)] * 2 + [(HD, 2 * QB)] * 2
    shapes = [(4,) + s for s in shapes]
    return pl.pallas_call(
        gate_kernel,
        grid=(2,),
        in_specs=[pl.BlockSpec(memory_space=pltpu.SMEM)]
        + [whole_spec(v.shape) for v in parts]
        + [pair_spec(wq.shape), pair_spec(wk.shape)],
        out_specs=[whole_spec(pack)] + [pair_spec(s) for s in shapes],
        out_shape=[jax.ShapeDtypeStruct(pack, BF16)]
        + [jax.ShapeDtypeStruct(s, F32 if i < 2 else BF16) for i, s in enumerate(shapes)],
        compiler_params=pltpu.CompilerParams(vmem_limit_bytes=VMEM),
        cost_estimate=pl.CostEstimate(flops=10 ** 10, bytes_accessed=10 ** 7, transcendentals=10 ** 6),
        name="gate",
    )(at, *parts, wq, wk)


def grads_kernel(y_ref, pack_ref, t_ref, gate_ref, log_ref, xh_ref, xl_ref, kh_ref, kl_ref, qh_ref, ql_ref, g_ref, loss_ref):
    gp = pl.program_id(0)
    wide = GROUP * HD
    for gg in range(2):
        g = gp * 2 + gg
        d_q, d_k = [], []
        for si in range(2):
            yy = y_ref[0] ^ si
            teacher = jnp.concatenate(
                [
                    jnp.concatenate([t_ref[z, x, yy, 0, :, gg * 64:gg * 64 + 64] for z in range(4)], axis=1)
                    for x in range(4)
                ],
                axis=0,
            )
            target = teacher / teacher.sum(axis=1, keepdims=True)
            at = slice(si * QB, (si + 1) * QB)
            if si == 0:
                some = target > 0.0
                term = jnp.where(some, target * jnp.log(jnp.where(some, target, 1.0)), 0.0)
                term = term - target * log_ref[gg]
                loss = term.sum(axis=1, keepdims=True).sum(axis=0, keepdims=True) * (1.0 / QB)
                loss_ref[0, gg:gg + 1, :] = jnp.broadcast_to(loss, (1, 128))
            slope = split2((gate_ref[gg, at, :] - target) * (SCALE / QB))
            ks = slice(si * CB, (si + 1) * CB)
            d_q.append(mm3(slope, (kh_ref[gg, ks, :], kl_ref[gg, ks, :])))
            d_k.append(mm3((qh_ref[gg, :, at], ql_ref[gg, :, at]), slope))
        d_q = split2(jnp.concatenate(d_q, axis=0))
        g_ref[gg, :wide, :] = mm3((xh_ref[gg], xl_ref[gg]), d_q)
        d_k = jnp.concatenate(split2(jnp.concatenate(d_k, axis=1)), axis=0)
        rows = [
            jnp.concatenate([packed(pack_ref, si, pl.multiple_of(g * 64 + p * 16, 16)) for si in range(2)], axis=0)
            for p in range(4)
        ]
        ends = mm(d_k, jnp.concatenate(rows[:2], axis=1))
        mean = mm(d_k, jnp.concatenate(rows[2:], axis=1))
        ends = ends[:HD] + ends[HD:]
        mean = mean[:HD, :HD] + (mean[HD:, :HD] + mean[:HD, HD:])
        g_ref[gg, wide:wide + HD, :] = ends[:, :HD].T
        g_ref[gg, wide + HD:wide + 2 * HD, :] = ends[:, HD:].T
        g_ref[gg, wide + 2 * HD:, :] = mean.T


def gradients(y, pack, teachers, parts):
    out = (4, (GROUP + 3) * HD, HD)
    return pl.pallas_call(
        grads_kernel,
        grid=(2,),
        in_specs=[
            pl.BlockSpec(memory_space=pltpu.SMEM),
            whole_spec(pack.shape),
            pl.BlockSpec((4, 4, 2, 1, 8, 128), lambda g: (0, 0, 0, g, 0, 0)),
        ]
        + [pair_spec(v.shape) for v in parts],
        out_specs=[pair_spec(out), pl.BlockSpec((1, 2, 128), lambda g: (g, 0, 0))],
        out_shape=[jax.ShapeDtypeStruct(out, F32), jax.ShapeDtypeStruct((2, 2, 128), F32)],
        compiler_params=pltpu.CompilerParams(vmem_limit_bytes=VMEM),
        name="gradients",
    )(y, pack, teachers, *parts)


def add_kernel(a_ref, b_ref, q_ref, k_ref):
    wide = q_ref.shape[1]
    q_ref[...] = a_ref[:, :wide] + b_ref[:, :wide]
    k_ref[...] = a_ref[:, wide:] + b_ref[:, wide:]


def add_cores(a, b):
    wide = GROUP * HD
    shapes = [(4, wide, HD), (4, a.shape[1] - wide, HD)]
    return pl.pallas_call(
        add_kernel,
        grid=(2,),
        in_specs=[pair_spec(a.shape)] * 2,
        out_specs=[pair_spec(s) for s in shapes],
        out_shape=[jax.ShapeDtypeStruct(s, F32) for s in shapes],
        compiler_params=pltpu.CompilerParams(vmem_limit_bytes=VMEM),
        name="add_cores",
    )(a, b)


def shift(x, axis, by):
    return lax.ppermute(x, axis, [(i, (i + by) % 4) for i in range(4)])


def swap(x, axis):
    return lax.ppermute(x, axis, [(0, 1), (1, 0)])


def ring(v, axis):
    return [v, shift(v, axis, 1), shift(v, axis, -1), shift(v, axis, 2)]


def upward(parts):
    return [parts[0], parts[2], parts[3], parts[1]]


def per_device(queries, keys, start_block, lengths, gate_query, gate_key):
    del lengths
    z, x, y = lax.axis_index("z"), lax.axis_index("x"), lax.axis_index("y")
    q, k = queries[0], keys[0]
    start = start_block[0]
    half_q, half_k = 2 * GROUP * HD, 2 * HD
    q_parts = ring(q, "z")
    k_before, k_after = shift(k, "x", 1), shift(k, "x", -1)
    pack = pool(start_block, q, k)
    pack, k_before, k_after = lax.optimization_barrier((pack, k_before, k_after))
    pack = ring(jnp.stack([pack, swap(pack, "y")]), "x")
    offs = (0, 3, 1, 2)
    q_pos = [start + (i * 4 + x) * 2 for i in range(4)]
    k_pos = [(z * 4 + ((x + o) & 3)) * 16 for o in offs]
    ints = lambda *v: jnp.stack([jnp.asarray(i, jnp.int32) for i in v])
    q_at = [((z + o) & 3) * 128 for o in offs]
    pos = ints(*q_pos, *k_pos, *q_at)
    bm0, ml, qs = block_scores(pos, q_parts, [k], (0,))
    pack, bm0, k_last = lax.optimization_barrier((pack, bm0, k))
    k_far = shift(k_last, "x", 2)
    packs = upward(ring(jnp.stack(upward(pack)), "z"))
    bm1, ml = block_scores(pos, [qs], [k_before, k_after], (1, 2), [ml])
    bm2, ml = block_scores(pos, [qs], [k_far], (3,), [ml])
    mls = ring(ml, "z")
    packs, _ = lax.optimization_barrier((packs, ml))
    pack, *parts = gate_part(ints(z, x), packs, gate_query, gate_key)
    parts, mls = lax.optimization_barrier((parts, mls))
    teachers = teacher_blocks(ints(x), [bm0, bm1, bm2], mls, 32)
    teachers = lax.all_to_all(teachers, ("z", "x", "y"), 0, 0, tiled=True).reshape(4, 4, 2, 2, 8, 128)
    grads, loss = gradients(ints(y), pack, teachers, parts)
    grad_q, grad_k = add_cores(grads, swap(grads, "c"))
    return grad_q, grad_k, loss[:, :, 0].reshape(1, 4)


def solution(mesh):
    fine = Mesh(mesh.devices.reshape(4, 4, 2, 2, 2), ("z", "x", "h", "y", "c"))
    ctx, dp = ("z", "x"), ("y", "c")
    placed = (
        P(dp, ctx, "h"),
        P(dp, ctx, "h"),
        P(dp),
        P(dp),
        P("h", None, None),
        P("h", None, None),
    )
    return jax.shard_map(
        per_device,
        mesh=fine,
        in_specs=placed,
        out_specs=(P("h", None, None), P("h", None, None), P(dp, "h")),
        check_vma=False,
    )
```

```python
import functools
import itertools
import math

import jax
import jax.numpy as jnp
from jax import lax
from jax.experimental import pallas as pl
from jax.experimental.pallas import tpu as pltpu
from jax.sharding import Mesh, PartitionSpec as P

BLK = 64
GROUP = 5
HD = 128
QB = 32
CB = 256
NEG = -1e30
FLOOR = -1e20
KT = 512
KB = KT // BLK
SAFE = 100.0
SCALE = HD ** -0.5
SCALE2 = SCALE * math.log2(math.e)
VMEM = 56 * 2 ** 20
F32 = jnp.float32
BF16 = jnp.bfloat16
NT = (((1,), (1,)), ((), ()))
TN = (((0,), (0,)), ((), ()))
NN = (((1,), (0,)), ((), ()))
PQ_AT = 256
START_AT = PQ_AT + 80
PACK = START_AT + 16


def split2(x):
    hi = x.astype(BF16)
    return hi, (x - hi.astype(F32)).astype(BF16)


def mm(a, b, dims=NN):
    return lax.dot_general(a, b, dims, preferred_element_type=F32)


def mm3(a, b, dims=NN):
    return mm(a[0], b[0], dims) + (mm(a[0], b[1], dims) + mm(a[1], b[0], dims))


def block_tops(s):
    return s.reshape(s.shape[0] // BLK, 8, 8, s.shape[1]).max(axis=1).max(axis=1)


def part_sums(s, m):
    return jnp.exp2(s - m).reshape(s.shape[0] // 8, 8, s.shape[1]).sum(axis=0)


def scores_kernel(pos_ref, *refs, n_q, shards):
    refs, nk = list(refs), len(shards)
    take = lambda n: [refs.pop(0) for _ in range(n)]
    q_refs, k_refs = take(n_q), take(nk)
    first = n_q > 1
    ml_in = [] if first else take(1)
    bm_ref, ml_ref = take(2)
    qs = take(1)[0] if first else q_refs[0]
    d_s, bad_s = refs
    rt, piece = qs.shape[2], k_refs[0].shape[0]
    q_pos = [pos_ref[i] for i in range(4)]
    kp = [pos_ref[4 + i] for i in shards]
    if first:
        for i, r in enumerate(q_refs):
            at = pl.multiple_of(pos_ref[8 + i], 128)
            for h in range(GROUP):
                hi, lo = split2(r[:, h * HD:(h + 1) * HD].astype(F32) * SCALE2)
                qs[0, h, pl.ds(at, 128), :] = jnp.concatenate([hi, lo], axis=1)
    tiles = [(p, o) for p in range(nk) for o in range(0, piece, KT)]
    low, high = functools.reduce(jnp.minimum, q_pos), functools.reduce(jnp.maximum, q_pos)
    full = [k + piece // BLK - 1 < low for k in kp]
    none = functools.reduce(jnp.minimum, kp) > high + 1

    def scores(t, h):
        p, o = tiles[t]
        k = k_refs[p][o:o + KT, :]
        return mm(jnp.concatenate([k, k], axis=1), qs[0, h], NT)

    def seen(p):
        lane = lax.broadcasted_iota(jnp.int32, (8, rt), 1)
        d = lane % 128 - lax.broadcasted_iota(jnp.int32, (8, rt), 0)
        for i, v in enumerate(q_pos):
            d = d + jnp.where(lane // 128 == i, (v - kp[p]) * BLK, 0)
        return d

    def masked(t, h):
        p, o = tiles[t]
        keep = jnp.concatenate([d_s[p] >= o + i for i in range(0, KT, 8)], axis=0)
        return jnp.where(keep, scores(t, h), NEG)

    def store(h, found):
        if ml_in:
            m = ml_in[0][0, h, 0:1, :]
            found = found + [(m, m, ml_in[0][0, h, 1:2, :])]
        big = functools.reduce(jnp.maximum, [f[1] for f in found])
        ml_ref[0, h, 0:1, :] = big
        ml_ref[0, h, 1:2, :] = sum(f[2] * jnp.exp2(f[0] - big) for f in found)

    def heads(masks):
        for p in range(nk):
            if masks[p]:
                d_s[p] = seen(p)

        def head(h, worst):
            found = []
            for t, (p, o) in enumerate(tiles):
                s = masked(t, h) if masks[p] else scores(t, h)
                if t == 0 or (o == 0 and (masks[p] or masks[p - 1])):
                    m = s[:BLK].reshape(8, 8, rt).max(axis=0).max(axis=0, keepdims=True)
                    m = jnp.maximum(m, FLOOR) if masks[p] else m
                    found.append([m, m, None])
                top, part = block_tops(s), part_sums(s, m)
                bm_ref[0, h, t * KB:(t + 1) * KB, :] = top
                f = found[-1]
                f[1] = jnp.maximum(f[1], top.max(axis=0, keepdims=True))
                f[2] = part if f[2] is None else f[2] + part
            store(h, [(f[0], f[1], f[2].sum(axis=0, keepdims=True)) for f in found])
            return functools.reduce(jnp.maximum, [f[1] - f[0] for f in found], worst)

        worst = jnp.zeros((1, rt), F32)
        if nk == 1 or not all(masks):
            for h in range(GROUP):
                worst = head(h, worst)
        else:
            worst = lax.fori_loop(0, GROUP, head, worst)
        bad_s[0] = jnp.max(worst)

    for masks in itertools.product((False, True), repeat=nk):
        match = functools.reduce(jnp.logical_and, [f != m for f, m in zip(full, masks)])
        pl.when(match & jnp.logical_not(none))(functools.partial(heads, masks))

    @pl.when(none)
    def _():
        bm_ref[...] = jnp.full(bm_ref.shape, NEG, F32)
        for h in range(GROUP):
            store(h, [(jnp.full((1, rt), FLOOR, F32), jnp.full((1, rt), FLOOR, F32), jnp.zeros((1, rt), F32))])
        bad_s[0] = 0.0

    @pl.when(bad_s[0] > SAFE)
    def _():
        for p in range(nk):
            d_s[p] = seen(p)

        def head(h, _):
            m, l = jnp.full((1, rt), FLOOR, F32), jnp.zeros((8, rt), F32)
            for t in range(len(tiles)):
                s = masked(t, h)
                top = block_tops(s)
                bm_ref[0, h, t * KB:(t + 1) * KB, :] = top
                new = jnp.maximum(m, top.max(axis=0, keepdims=True))
                l = l * jnp.exp2(m - new) + part_sums(s, new)
                m = new
            store(h, [(m, m, l.sum(axis=0, keepdims=True))])
            return 0

        lax.fori_loop(0, GROUP, head, 0)


def block_scores(pos, q_parts, k_parts, shards, ml_in=()):
    first = len(q_parts) > 1
    rt, kn = 512, sum(k.shape[0] for k in k_parts)
    groups = k_parts[0].shape[1] // HD
    per_group = lambda s: pl.BlockSpec((1,) + tuple(s[1:]), lambda g, p: (g, 0, 0, 0))
    lanes = lambda v: pl.BlockSpec((v.shape[0], v.shape[1] // groups), lambda g, p: (0, g))
    shapes = [(groups, GROUP, kn // BLK, rt), (groups, GROUP, 2, rt)] + [(groups, GROUP, rt, 2 * HD)] * first
    return pl.pallas_call(
        functools.partial(scores_kernel, n_q=len(q_parts), shards=shards),
        grid_spec=pltpu.PrefetchScalarGridSpec(
            num_scalar_prefetch=1,
            grid=(groups,),
            in_specs=[lanes(q) if first else per_group(q.shape) for q in q_parts]
            + [lanes(k) for k in k_parts]
            + [per_group(m.shape) for m in ml_in],
            out_specs=[per_group(s) for s in shapes],
            scratch_shapes=[pltpu.VMEM((len(k_parts), 8, rt), jnp.int32), pltpu.SMEM((1,), F32)],
        ),
        out_shape=[jax.ShapeDtypeStruct(s, t) for s, t in zip(shapes, (F32, F32, BF16))],
        compiler_params=pltpu.CompilerParams(vmem_limit_bytes=VMEM),
        name="block_scores",
    )(pos, *q_parts, *k_parts, *ml_in)


def pool_kernel(start_ref, q_ref, k_ref, out_ref):
    groups = k_ref.shape[1] // HD
    for g in range(groups):
        x = k_ref[:, g * HD:(g + 1) * HD].astype(F32).reshape(16, BLK, HD)
        hi, lo = split2(x.sum(axis=1) * (1.0 / BLK))
        parts = [x.max(axis=1).astype(BF16), x.min(axis=1).astype(BF16), hi, lo]
        for p, part in enumerate(parts):
            out_ref[g * 64 + p * 16:g * 64 + p * 16 + 16, :] = part
    for p in range(GROUP):
        rows = []
        for g in range(groups):
            at = (g * GROUP + p) * HD
            x = q_ref[:, at:at + HD].astype(F32).reshape(2, BLK, HD)
            rows.append(x.sum(axis=1) * (1.0 / BLK))
        hi, lo = split2(jnp.concatenate(rows, axis=0))
        at = PQ_AT + p * 16
        out_ref[at:at + 16, :] = jnp.concatenate([hi.astype(F32), lo.astype(F32)], axis=0).astype(BF16)
    out_ref[START_AT:, :] = jnp.full((16, HD), start_ref[0].astype(F32), F32).astype(BF16)


def pool(start_block, q, k):
    return pl.pallas_call(
        pool_kernel,
        in_specs=[
            pl.BlockSpec(memory_space=pltpu.SMEM),
            pl.BlockSpec(memory_space=pltpu.VMEM),
            pl.BlockSpec(memory_space=pltpu.VMEM),
        ],
        out_specs=pl.BlockSpec(memory_space=pltpu.VMEM),
        out_shape=jax.ShapeDtypeStruct((PACK, HD), BF16),
        compiler_params=pltpu.CompilerParams(vmem_limit_bytes=VMEM),
        name="pool",
    )(start_block, q, k)


def teacher_kernel(x_ref, *refs):
    near, sides, far = refs[:3]
    ml_refs, (out_ref, sc) = refs[3:-2], refs[-2:]
    rt = near.shape[3]
    to = [pl.multiple_of(((x_ref[0] + o) & 3) * 16, 16) for o in (0, 3, 1, 2)]
    for g in range(4):
        for h in range(GROUP):
            ms = [m[g, h, 0:1, :] for m in ml_refs]
            m = functools.reduce(jnp.maximum, ms)
            l = sum(ref[g, h, 1:2, :] * jnp.exp2(mi - m) for ref, mi in zip(ml_refs, ms))
            lse = m + jnp.log(l) * math.log2(math.e)
            parts = [near[g, h], sides[g, h, :16], sides[g, h, 16:], far[g, h]]
            for at, v in zip(to, parts):
                sc[g // 2 * GROUP + h, pl.ds(at + g % 2 * 64, 16), :] = v - lse
    for gp in range(2):
        totals = [None] * (rt // 128)
        for h in range(GROUP):
            for i in range(rt // 128):
                t = sc[gp * GROUP + h, :, i * 128:(i + 1) * 128].T
                top = jnp.exp2(t.reshape(2, BLK, 128).max(axis=1))
                totals[i] = top if h == 0 else totals[i] + top
        tile = jnp.concatenate(totals, axis=0) * (1.0 / GROUP)
        out_ref[:, gp] = jnp.broadcast_to(tile[None], (out_ref.shape[0],) + tile.shape)


def teacher_blocks(x, bms, mls, copies):
    return pl.pallas_call(
        teacher_kernel,
        in_specs=[pl.BlockSpec(memory_space=pltpu.SMEM)]
        + [pl.BlockSpec(memory_space=pltpu.VMEM)] * (len(bms) + len(mls)),
        out_specs=pl.BlockSpec(memory_space=pltpu.VMEM),
        out_shape=jax.ShapeDtypeStruct((copies, 2, 8, 128), F32),
        scratch_shapes=[pltpu.VMEM((2 * GROUP, 128, bms[0].shape[3]), F32)],
        compiler_params=pltpu.CompilerParams(vmem_limit_bytes=VMEM),
        name="teacher",
    )(x, *bms, *mls)


def packed(pack_ref, si, at):
    return pack_ref[:, :, si, pl.ds(at, 16), :].reshape(CB, HD)


def gate_kernel(at_ref, *refs):
    parts, (wq_ref, wk_ref) = refs[:4], refs[4:6]
    pack_ref, gate_ref, log_ref, xh_ref, xl_ref, kh_ref, kl_ref, qh_ref, ql_ref = refs[6:]
    gp = pl.program_id(0)

    @pl.when(gp == 0)
    def _():
        for i in range(4):
            for j in range(4):
                for si in range(2):
                    pack_ref[(at_ref[0] + i) & 3, (at_ref[1] + j) & 3, si] = parts[i][j, si]

    row = lax.broadcasted_iota(jnp.int32, (2 * QB, CB), 0)
    col = lax.broadcasted_iota(jnp.int32, (2 * QB, CB), 1)
    a = row % QB
    pick = (
        (col % 8 == (gp * 2 + row // QB) * 2 + a % 2)
        & (col // 16 % 4 == a // 8)
        & (col // 64 == a % 8 // 2)
    )
    pick = jnp.where(pick, 1.0, 0.0).astype(BF16)
    a = a[:QB]
    ahead = (col[:QB] - (a % 8 // 2 * 8 + a // 8 * 2 + a % 2)).astype(F32)
    wq = jnp.concatenate([wq_ref[0], wq_ref[1]], axis=1)
    xs, qs = [[], []], [[], []]
    for si in range(2):
        rows = jnp.concatenate([packed(pack_ref, si, PQ_AT + p * 16) for p in range(GROUP)], axis=1)
        raw = split2(mm(rows, wq))
        both = mm(pick, rows)
        start = pack_ref[0, 0, si, START_AT:START_AT + 16, :].astype(F32)[0:1, 0:1]
        live = ahead <= start
        for gg in range(2):
            g = gp * 2 + gg
            ks = [packed(pack_ref, si, pl.multiple_of(g * 64 + p * 16, 16)) for p in range(4)]
            mean = wk_ref[gg, 2 * HD:, :]
            proj_k = mm(jnp.concatenate(ks[:2], axis=1), wk_ref[gg, :2 * HD, :])
            proj_k = proj_k + mm(jnp.concatenate(ks[2:], axis=1), jnp.concatenate([mean, mean], axis=0))
            xs[gg].append(both[gg * QB:(gg + 1) * QB])
            mine, lanes = pick[gg * QB:(gg + 1) * QB], slice(gg * HD, (gg + 1) * HD)
            proj_q = mm(mine, raw[0][:, lanes]) + mm(mine, raw[1][:, lanes])
            qs[gg].append(proj_q)
            proj_k = split2(proj_k)
            kh_ref[gg, si * CB:(si + 1) * CB, :] = proj_k[0]
            kl_ref[gg, si * CB:(si + 1) * CB, :] = proj_k[1]
            logits = mm3(split2(proj_q), proj_k, NT) * SCALE
            masked = jnp.where(live, logits, NEG)
            top = masked.max(axis=1, keepdims=True)
            ex = jnp.where(live, jnp.exp(masked - top), 0.0)
            total = ex.sum(axis=1, keepdims=True)
            gate_ref[gg, si * QB:(si + 1) * QB, :] = ex / total
            if si == 0:
                log_ref[gg] = jnp.where(live, masked - top - jnp.log(total), 0.0)
    for gg in range(2):
        hi, lo = split2(jnp.concatenate(xs[gg], axis=0).T)
        xh_ref[gg] = hi
        xl_ref[gg] = lo
        hi, lo = split2(jnp.concatenate(qs[gg], axis=0).T)
        qh_ref[gg] = hi
        ql_ref[gg] = lo


def pair_spec(shape):
    return pl.BlockSpec((2,) + tuple(shape[1:]), lambda g: (g,) + (0,) * (len(shape) - 1))


def whole_spec(shape):
    return pl.BlockSpec(tuple(shape), lambda g: (0,) * len(shape))


def gate_part(at, parts, wq, wk):
    pack = (4, 4, 2, PACK, HD)
    shapes = [(2 * QB, CB), (QB, CB)] + [(GROUP * HD, 2 * QB)] * 2 + [(2 * CB, HD)] * 2 + [(HD, 2 * QB)] * 2
    shapes = [(4,) + s for s in shapes]
    return pl.pallas_call(
        gate_kernel,
        grid=(2,),
        in_specs=[pl.BlockSpec(memory_space=pltpu.SMEM)]
        + [whole_spec(v.shape) for v in parts]
        + [pair_spec(wq.shape), pair_spec(wk.shape)],
        out_specs=[whole_spec(pack)] + [pair_spec(s) for s in shapes],
        out_shape=[jax.ShapeDtypeStruct(pack, BF16)]
        + [jax.ShapeDtypeStruct(s, F32 if i < 2 else BF16) for i, s in enumerate(shapes)],
        compiler_params=pltpu.CompilerParams(vmem_limit_bytes=VMEM),
        cost_estimate=pl.CostEstimate(flops=10 ** 10, bytes_accessed=10 ** 7, transcendentals=10 ** 6),
        name="gate",
    )(at, *parts, wq, wk)


def grads_kernel(y_ref, pack_ref, t_ref, gate_ref, log_ref, xh_ref, xl_ref, kh_ref, kl_ref, qh_ref, ql_ref, g_ref, loss_ref):
    gp = pl.program_id(0)
    wide = GROUP * HD
    for gg in range(2):
        g = gp * 2 + gg
        d_q, d_k = [], []
        for si in range(2):
            yy = y_ref[0] ^ si
            teacher = jnp.concatenate(
                [
                    jnp.concatenate([t_ref[z, x, yy, 0, :, gg * 64:gg * 64 + 64] for z in range(4)], axis=1)
                    for x in range(4)
                ],
                axis=0,
            )
            target = teacher / teacher.sum(axis=1, keepdims=True)
            at = slice(si * QB, (si + 1) * QB)
            if si == 0:
                some = target > 0.0
                term = jnp.where(some, target * jnp.log(jnp.where(some, target, 1.0)), 0.0)
                term = term - target * log_ref[gg]
                loss = term.sum(axis=1, keepdims=True).sum(axis=0, keepdims=True) * (1.0 / QB)
                loss_ref[0, gg:gg + 1, :] = jnp.broadcast_to(loss, (1, 128))
            slope = split2((gate_ref[gg, at, :] - target) * (SCALE / QB))
            ks = slice(si * CB, (si + 1) * CB)
            d_q.append(mm3(slope, (kh_ref[gg, ks, :], kl_ref[gg, ks, :])))
            d_k.append(mm3((qh_ref[gg, :, at], ql_ref[gg, :, at]), slope))
        d_q = split2(jnp.concatenate(d_q, axis=0))
        g_ref[gg, :wide, :] = mm3((xh_ref[gg], xl_ref[gg]), d_q)
        d_k = jnp.concatenate(split2(jnp.concatenate(d_k, axis=1)), axis=0)
        rows = [
            jnp.concatenate([packed(pack_ref, si, pl.multiple_of(g * 64 + p * 16, 16)) for si in range(2)], axis=0)
            for p in range(4)
        ]
        ends = mm(d_k, jnp.concatenate(rows[:2], axis=1))
        mean = mm(d_k, jnp.concatenate(rows[2:], axis=1))
        ends = ends[:HD] + ends[HD:]
        mean = mean[:HD, :HD] + (mean[HD:, :HD] + mean[:HD, HD:])
        g_ref[gg, wide:wide + HD, :] = ends[:, :HD].T
        g_ref[gg, wide + HD:wide + 2 * HD, :] = ends[:, HD:].T
        g_ref[gg, wide + 2 * HD:, :] = mean.T


def gradients(y, pack, teachers, parts):
    out = (4, (GROUP + 3) * HD, HD)
    return pl.pallas_call(
        grads_kernel,
        grid=(2,),
        in_specs=[
            pl.BlockSpec(memory_space=pltpu.SMEM),
            whole_spec(pack.shape),
            pl.BlockSpec((4, 4, 2, 1, 8, 128), lambda g: (0, 0, 0, g, 0, 0)),
        ]
        + [pair_spec(v.shape) for v in parts],
        out_specs=[pair_spec(out), pl.BlockSpec((1, 2, 128), lambda g: (g, 0, 0))],
        out_shape=[jax.ShapeDtypeStruct(out, F32), jax.ShapeDtypeStruct((2, 2, 128), F32)],
        compiler_params=pltpu.CompilerParams(vmem_limit_bytes=VMEM),
        name="gradients",
    )(y, pack, teachers, *parts)


def add_kernel(a_ref, b_ref, q_ref, k_ref):
    wide = q_ref.shape[1]
    q_ref[...] = a_ref[:, :wide] + b_ref[:, :wide]
    k_ref[...] = a_ref[:, wide:] + b_ref[:, wide:]


def add_cores(a, b):
    wide = GROUP * HD
    shapes = [(4, wide, HD), (4, a.shape[1] - wide, HD)]
    return pl.pallas_call(
        add_kernel,
        grid=(2,),
        in_specs=[pair_spec(a.shape)] * 2,
        out_specs=[pair_spec(s) for s in shapes],
        out_shape=[jax.ShapeDtypeStruct(s, F32) for s in shapes],
        compiler_params=pltpu.CompilerParams(vmem_limit_bytes=VMEM),
        name="add_cores",
    )(a, b)


def shift(x, axis, by):
    return lax.ppermute(x, axis, [(i, (i + by) % 4) for i in range(4)])


def swap(x, axis):
    return lax.ppermute(x, axis, [(0, 1), (1, 0)])


def ring(v, axis):
    return [v, shift(v, axis, 1), shift(v, axis, -1), shift(v, axis, 2)]


def upward(parts):
    return [parts[0], parts[2], parts[3], parts[1]]


def per_device(queries, keys, start_block, lengths, gate_query, gate_key):
    del lengths
    z, x, y = lax.axis_index("z"), lax.axis_index("x"), lax.axis_index("y")
    q, k = queries[0], keys[0]
    start = start_block[0]
    half_q, half_k = 2 * GROUP * HD, 2 * HD
    q_parts = ring(q, "z")
    k_before, k_after = shift(k, "x", 1), shift(k, "x", -1)
    pack = pool(start_block, q, k)
    pack, k_before, k_after = lax.optimization_barrier((pack, k_before, k_after))
    pack = ring(jnp.stack([pack, swap(pack, "y")]), "x")
    offs = (0, 3, 1, 2)
    q_pos = [start + (i * 4 + x) * 2 for i in range(4)]
    k_pos = [(z * 4 + ((x + o) & 3)) * 16 for o in offs]
    ints = lambda *v: jnp.stack([jnp.asarray(i, jnp.int32) for i in v])
    q_at = [((z + o) & 3) * 128 for o in offs]
    pos = ints(*q_pos, *k_pos, *q_at)
    bm0, ml, qs = block_scores(pos, q_parts, [k], (0,))
    pack, bm0, k_last = lax.optimization_barrier((pack, bm0, k))
    k_far = shift(k_last, "x", 2)
    packs = upward(ring(jnp.stack(upward(pack)), "z"))
    bm1, ml = block_scores(pos, [qs], [k_before, k_after], (1, 2), [ml])
    bm2, ml = block_scores(pos, [qs], [k_far], (3,), [ml])
    mls = ring(ml, "z")
    packs, _ = lax.optimization_barrier((packs, ml))
    pack, *parts = gate_part(ints(z, x), packs, gate_query, gate_key)
    parts, mls = lax.optimization_barrier((parts, mls))
    teachers = teacher_blocks(ints(x), [bm0, bm1, bm2], mls, 32)
    teachers = lax.all_to_all(teachers, ("z", "x", "y"), 0, 0, tiled=True).reshape(4, 4, 2, 2, 8, 128)
    grads, loss = gradients(ints(y), pack, teachers, parts)
    grad_q, grad_k = add_cores(grads, swap(grads, "c"))
    return grad_q, grad_k, loss[:, :, 0].reshape(1, 4)


def solution(mesh):
    fine = Mesh(mesh.devices.reshape(4, 4, 2, 2, 2), ("z", "x", "h", "y", "c"))
    ctx, dp = ("z", "x"), ("y", "c")
    placed = (
        P(dp, ctx, "h"),
        P(dp, ctx, "h"),
        P(dp),
        P(dp),
        P("h", None, None),
        P("h", None, None),
    )
    return jax.shard_map(
        per_device,
        mesh=fine,
        in_specs=placed,
        out_specs=(P("h", None, None), P("h", None, None), P(dp, "h")),
        check_vma=False,
    )
```
